256 devices in a mesh: section: 16 (over z_hi, y), dp: 16 (over x, z_lo, core).
Axes of the slice: x: 4, y: 4, z: 8 (z_hi: 4, z_lo: 2; z = z_hi * 2 + z_lo), core: 2. Of those that a mesh axis runs over, the one named last changes fastest.
Arguments:
- acts: bfloat16 [16, 4, 512, 4096], P('section', None, 'dp'), may hold values from -6 to 6
- out_grad: bfloat16 [4, 512, 4096], P(None, 'dp'), may hold values from -6 to 6
- w_in: bfloat16 [16, 4096, 1152], P('section', 'dp'), may hold values from -0.09375 to 0.09375
- w_out: bfloat16 [16, 4096, 384], P('section', 'dp'), may hold values from -0.09375 to 0.09375
- decay_rate: float32 [16, 3], P('section'), may hold values from 0.004 to 0.04
- cycle_order: int32 [16], replicated, may hold values from 0 to 15, each once
Outputs:
- in_grad: bfloat16 [16, 4, 512, 4096], P('section', None, 'dp')
- grad_in: float32 [16, 4096, 1152], P('section', 'dp')
- grad_out: float32 [16, 4096, 384], P('section', 'dp')
The draws below stay inside these ranges and needn't reach their ends.
Inputs may be any that keep to these rules, and one draw needn't show every extreme that they name: `cycle_order`: a permutation of the 16 replicas.
All inputs are finite; a program needn't handle non-finite values.
Results may differ from the reference program's by a relative error of at most 0.038.
Values may be sent and summed in bfloat16 or wider, within the bound.
A program may use at most 192 MiB of HBM per device.

```python
import math
import jax
import jax.numpy as jnp
from jax import lax

D = 4096
H = 3
HD = 128
TOK = 32
MICRO = 4
TOKENS = 512
N_SECTION = 16
N_DP = 16


def raised(entries, rng, source, target, shards_of, factor):
    def block_of(axis_at):
        return (jnp.arange(entries.shape[axis_at]) // (entries.shape[axis_at] // shards_of)).reshape((-1,) + (1,) * (entries.ndim - 1 - axis_at))

    first = jax.random.permutation(rng, shards_of)[block_of(target)]
    other_side = (block_of(target) + shards_of // 2) % shards_of
    return jnp.where((block_of(source) == first) | (block_of(source) == other_side), factor * entries, entries)


def shard_levels(key, dims, split, smallest, top_value):
    loudness, own = 1.0, jax.random.fold_in(key, 6)
    for dim, parts in split:
        heights = jnp.exp(jax.random.uniform(jax.random.fold_in(own, dim), (parts,), jnp.float32, smallest / len(split), top_value / len(split)))
        loudness = loudness * jnp.repeat(heights, dims[dim] // parts).reshape([-1 if axis == dim else 1 for axis in range(len(dims))])
    return loudness


def noise(key, extent, spread, most, cuts=(), dtype=jnp.bfloat16):
    array = spread * jax.random.normal(key, extent, jnp.float32)
    if cuts:
        array = array * shard_levels(key, extent, cuts, -0.22, 0.18)
    return jnp.clip(array, -most, most).astype(dtype)


def noise_with(stream_key, shape, spread, bound, shards, heavy, dtype=jnp.bfloat16):
    array = spread * jax.random.normal(stream_key, shape, jnp.float32)
    if shards:
        array = array * shard_levels(stream_key, shape, shards, -0.22, 0.18)
    return jnp.clip(raised(array, jax.random.fold_in(stream_key, 3), *heavy), -bound, bound).astype(dtype)


def setup_inputs(seed: int = 0) -> dict:
    arg_keys = jax.random.split(jax.random.key(seed), 7)
    acts = noise_with(arg_keys[0], (N_SECTION, MICRO, TOKENS, D), 1.0, 6.0, ((0, 16), (2, 16)), (2, 3, 16, 2.0))
    out_grad = noise(arg_keys[1], (MICRO, TOKENS, D), 1.0, 6.0, ((1, 16),))
    w_in = noise(arg_keys[2], (N_SECTION, D, 3 * H * HD), D ** -0.5, 0.09375, ((0, 16), (1, 16)))
    w_out = noise(arg_keys[3], (N_SECTION, D, H * HD), D ** -0.5, 0.09375, ((0, 16), (1, 16)))
    decay_rate = jnp.clip(jnp.exp(math.log(0.04) - 2.30258502 * jax.random.uniform(arg_keys[4], (N_SECTION, H), jnp.float32) ** shard_levels(arg_keys[4], (N_SECTION, H), ((0, 16),), -0.2, 0.2)), 0.004, 0.04)
    cycle_order = jax.random.permutation(arg_keys[5], N_DP).astype(jnp.int32)
    return {"acts": acts, "out_grad": out_grad, "w_in": w_in, "w_out": w_out, "decay_rate": decay_rate, "cycle_order": cycle_order}


def decay_table(rates, length):
    spots = jnp.arange(length).astype(jnp.float32)
    offset = spots[:, None] - spots[None, :]
    decayed = jnp.exp(-rates[:, None, None] * jnp.maximum(offset, 0.0)[None])
    return jnp.where(offset[None] >= 0.0, decayed, 0.0).astype(jnp.float32)


def retention_back(inputs, grad_y, weight_in, weight_out, table):
    copies, length, width = inputs.shape
    cols = H * HD
    qkv = jnp.dot(inputs.reshape(copies * length, width), weight_in, preferred_element_type=jnp.float32)
    qkv = qkv.astype(jnp.bfloat16).reshape(copies, length, 3 * cols)
    query = qkv[:, :, :cols].reshape(copies, length, H, HD).astype(jnp.float32)
    keys = qkv[:, :, cols:2 * cols].reshape(copies, length, H, HD).astype(jnp.float32)
    values = qkv[:, :, 2 * cols:].reshape(copies, length, H, HD).astype(jnp.float32)
    scores = (jnp.einsum('rthe,rjhe->rhtj', query, keys) * table / HD).astype(jnp.bfloat16).astype(jnp.float32)
    mixed = jnp.einsum('rhtj,rjhe->rthe', scores, values).reshape(copies, length, cols).astype(jnp.bfloat16)
    d_mixed = jnp.dot(grad_y.reshape(copies * length, width), weight_out, preferred_element_type=jnp.float32)
    d_mixed = d_mixed.astype(jnp.bfloat16).reshape(copies, length, H, HD).astype(jnp.float32)
    d_scores = (jnp.einsum('rthe,rjhe->rhtj', d_mixed, values) * table / HD).astype(jnp.bfloat16).astype(jnp.float32)
    d_query = jnp.einsum('rhtj,rjhe->rthe', d_scores, keys).reshape(copies, length, cols)
    d_keys = jnp.einsum('rhtj,rthe->rjhe', d_scores, query).reshape(copies, length, cols)
    d_values = jnp.einsum('rhtj,rthe->rjhe', scores, d_mixed).reshape(copies, length, cols)
    d_all = jnp.concatenate([d_query, d_keys, d_values], axis=2).astype(jnp.bfloat16)
    back = jnp.dot(d_all.reshape(copies * length, 3 * cols), weight_in.T, preferred_element_type=jnp.float32)
    d_input = (grad_y.astype(jnp.float32) + back.reshape(copies, length, width)).astype(jnp.bfloat16)
    return d_input, d_all, mixed


def shrink(total, live):
    scaled = (total * live[:, None, None]).astype(jnp.bfloat16)
    scaled = lax.optimization_barrier(scaled)
    return jnp.sum(scaled.astype(jnp.float32), axis=0) / (N_DP - 1.0)


def reference(acts, out_grad, w_in, w_out, decay_rate, cycle_order):
    live = jnp.where(jnp.arange(N_DP) == cycle_order[N_DP - 1], 0.0, 1.0).astype(jnp.float32)
    cols = H * HD
    current = out_grad
    in_list = [None] * N_SECTION
    gin_list = [None] * N_SECTION
    gout_list = [None] * N_SECTION
    for section in range(N_SECTION - 1, -1, -1):
        table = decay_table(decay_rate[section], TOK)
        total_in = jnp.zeros((N_DP, D, 3 * cols), jnp.float32)
        total_out = jnp.zeros((N_DP, D, cols), jnp.float32)
        results = []
        for which in range(MICRO):
            inputs = acts[section, which].reshape(N_DP, TOK, D)
            grad_y = current[which].reshape(N_DP, TOK, D)
            d_input, d_all, mixed = retention_back(inputs, grad_y, w_in[section], w_out[section], table)
            total_in = total_in + jnp.einsum('rtd,rtc->rdc', inputs.astype(jnp.float32), d_all.astype(jnp.float32))
            total_out = total_out + jnp.einsum('rtd,rtc->rdc', grad_y.astype(jnp.float32), mixed.astype(jnp.float32))
            results.append(d_input.reshape(TOKENS, D))
        current = jnp.stack(results)
        in_list[section] = current
        gin_list[section] = shrink(total_in, live)
        gout_list[section] = shrink(total_out, live)
    return jnp.stack(in_list), jnp.stack(gin_list), jnp.stack(gout_list)
```

```python
import functools

import jax
import jax.numpy as jnp
from jax import lax
from jax.experimental import pallas as pl
from jax.experimental.pallas import tpu as pltpu
from jax.sharding import PartitionSpec as P

MESH = pl.DeviceIdType.MESH
BF = jnp.bfloat16
F32 = jnp.float32


def dot(a, b):
    return jnp.dot(a, b, preferred_element_type=F32)


def dot_nt(a, b):
    return lax.dot_general(a, b, (((1,), (1,)), ((), ())), preferred_element_type=F32)


def dot_tn(a, b):
    return lax.dot_general(a, b, (((0,), (0,)), ((), ())), preferred_element_type=F32)


def kernel(
    dims,
    acts, out_grad, w_in, w_out, rates, order,
    in_grad, grad_in, grad_out,
    WI, WO, XB, DY, NX, ACC, QKV, SC, DR, TAB, XS, DS, DQ, RA, GI, GO,
    loc, wsend, wrecv, csend, crecv, xsend, xrecv, rsend, rrecv, qsend, qrecv, ysend, yrecv, outsem,
):
    nsec, ndp, micro, tok, width, heads, hd, nchunk = dims
    cols = heads * hd
    blk = width // ndp
    half = blk // 2
    per = ndp // nchunk
    nx = ndp // 4
    s = lax.axis_index("section")
    r = lax.axis_index("dp")
    x, zl, c = r // 4, (r // 2) % 2, r % 2
    last = nsec - 1
    slot = c * (ndp // 2) + r // 2

    def rep(xx, zz, cc):
        return lax.rem(xx + nx, nx) * 4 + zz * 2 + cc

    core, zp = rep(x, zl, 1 - c), rep(x, 1 - zl, c)
    xp, xm, xo = rep(x + 1, zl, c), rep(x - 1, zl, c), rep(x + 2, zl, c)
    xpz, xmz, xoz = rep(x + 1, 1 - zl, c), rep(x - 1, 1 - zl, c), rep(x + 2, 1 - zl, c)

    def peer(i):
        return lax.rem(r + i, ndp)

    def slot_of(q):
        return lax.rem(q, 2) * (ndp // 2) + q // 2

    local = [
        pltpu.make_async_copy(w_in.at[0], WI.at[r], loc.at[0]),
        pltpu.make_async_copy(w_out.at[0], WO.at[r], loc.at[1]),
    ]
    for i in range(ndp):
        local.append(
            pltpu.make_async_copy(
                acts.at[0, :, :, pl.ds(i * blk, blk)], XB.at[i], loc.at[2 + i]
            )
        )
    for copy in local:
        copy.start()

    barrier = pltpu.get_barrier_semaphore()
    for i in range(1, ndp):
        pl.semaphore_signal(barrier, inc=1, device_id=(s, peer(i)), device_id_type=MESH)

    @pl.when(s > 0)
    def _():
        pl.semaphore_signal(barrier, inc=1, device_id=(s - 1, r), device_id_type=MESH)

    @pl.when(s < last)
    def _():
        pl.semaphore_signal(barrier, inc=1, device_id=(s + 1, r), device_id_type=MESH)

    neighbours = jnp.where(s > 0, 1, 0) + jnp.where(s < last, 1, 0)
    pl.semaphore_wait(barrier, ndp - 1 + neighbours)

    def piece(ref, q, h):
        return ref.at[q, pl.ds(h * half, half)]

    sent = []

    def push(q, h, target, own=False):
        for which, ref in enumerate((WI, WO)):
            if own:
                src = (w_in, w_out)[which].at[0, pl.ds(h * half, half)]
            else:
                src = piece(ref, q, h)
            copy = pltpu.make_async_remote_copy(
                src_ref=src,
                dst_ref=piece(ref, q, h),
                send_sem=wsend.at[len(sent)],
                recv_sem=wrecv.at[q, h, which],
                device_id=(s, target),
                device_id_type=MESH,
            )
            copy.start()
            sent.append(copy)

    def arrive(q, h):
        for which, ref in enumerate((WI, WO)):
            pltpu.make_async_remote_copy(
                src_ref=piece(ref, q, h),
                dst_ref=piece(ref, q, h),
                send_sem=wsend.at[0],
                recv_sem=wrecv.at[q, h, which],
                device_id=(s, core),
                device_id_type=MESH,
            ).wait_recv()

    for h in range(2):
        for target in (xp, xm, zp, core):
            push(r, h, target, own=True)

    ACC[...] = jnp.zeros_like(ACC)

    def add(q):
        ACC[...] += dot(XB[q].reshape(micro * tok, blk), WI[q])

    for copy in local:
        copy.wait()

    @pl.when(s == last)
    def _():
        for i in range(ndp):
            pltpu.make_async_copy(
                out_grad.at[:, :, pl.ds(i * blk, blk)], DY.at[:, i], outsem.at[i]
            ).start()

    spot_t = lax.broadcasted_iota(jnp.int32, (tok, tok), 0)
    spot_j = lax.broadcasted_iota(jnp.int32, (tok, tok), 1)
    offset = (spot_t - spot_j).astype(F32)
    for h in range(heads):
        decayed = jnp.exp(-rates[0, h] * jnp.maximum(offset, 0.0))
        TAB[h] = jnp.where(offset >= 0.0, decayed, 0.0)

    add(r)
    arrive(xm, 0)
    push(xm, 0, xp)
    push(xm, 0, core)
    arrive(xp, 0)
    push(xp, 0, core)
    arrive(zp, 0)
    push(zp, 0, xp)
    push(zp, 0, xm)
    push(zp, 0, core)
    arrive(core, 0)
    arrive(core, 1)
    add(core)
    arrive(xp, 1)
    push(xp, 1, xm)
    push(xp, 1, core)
    arrive(xm, 1)
    push(xm, 1, core)
    arrive(zp, 1)
    push(zp, 1, xp)
    push(zp, 1, xm)
    push(zp, 1, core)
    add(xm)
    add(xp)
    add(zp)
    arrive(xo, 0)
    push(xo, 0, zp)
    push(xo, 0, core)
    arrive(xo, 1)
    push(xo, 1, zp)
    push(xo, 1, core)

    def other(q):
        return q + 1 - 2 * c

    for q in (xm, xp, zp):
        arrive(other(q), 0)
        arrive(other(q), 1)
        add(other(q))
    add(xo)
    for q in (xmz, xpz):
        for h in range(2):
            arrive(q, h)
            push(q, h, core)
    arrive(xoz, 0)
    push(xoz, 0, core)
    add(xmz)
    add(xpz)
    arrive(xoz, 1)
    push(xoz, 1, core)
    for q in (xo, xmz, xpz):
        arrive(other(q), 0)
        arrive(other(q), 1)
        add(other(q))
    add(xoz)
    arrive(other(xoz), 0)
    arrive(other(xoz), 1)
    add(other(xoz))

    failed = order[ndp - 1]
    live = jnp.where(r == failed, 0.0, 1.0).astype(F32)
    mine = pl.ds(pl.multiple_of(slot * tok, tok), tok)

    QKV[...] = ACC[...].astype(BF).reshape(micro, tok, 3 * cols)
    for m in range(micro):
        for h in range(heads):
            q = QKV[m, :, h * hd : (h + 1) * hd]
            k = QKV[m, :, cols + h * hd : cols + (h + 1) * hd]
            v = QKV[m, :, 2 * cols + h * hd : 2 * cols + (h + 1) * hd]
            score = (dot_nt(q, k) * TAB[h] / hd).astype(BF)
            SC[m, h] = score
            mixed = dot(score, v).astype(BF)
            RA[m, mine, h * hd : (h + 1) * hd] = (mixed.astype(F32) * live).astype(BF)

    plane = pl.ds(pl.multiple_of(c * (ndp // 2) * tok, tok), (ndp // 2) * tok)
    foreign = pl.ds(pl.multiple_of((1 - c) * (ndp // 2) * tok, tok), (ndp // 2) * tok)

    def rows_of(q):
        return pl.ds(pl.multiple_of(slot_of(q) * tok, tok), tok)

    def x_copy(i):
        q = peer(i)
        return pltpu.make_async_remote_copy(
            src_ref=XB.at[q], dst_ref=XS.at[:, mine],
            send_sem=xsend.at[i], recv_sem=xrecv.at[i],
            device_id=(s, q), device_id_type=MESH,
        )

    def x_wait(i):
        q = lax.rem(r - i + ndp, ndp)
        pltpu.make_async_remote_copy(
            src_ref=XB.at[q], dst_ref=XS.at[:, rows_of(q)],
            send_sem=xsend.at[i], recv_sem=xrecv.at[i],
            device_id=(s, q), device_id_type=MESH,
        ).wait_recv()

    def r_copy(i):
        q = peer(2 * i)
        return pltpu.make_async_remote_copy(
            src_ref=RA.at[:, mine], dst_ref=RA.at[:, mine],
            send_sem=rsend.at[i], recv_sem=rrecv.at[i],
            device_id=(s, q), device_id_type=MESH,
        )

    def r_wait(i):
        q = lax.rem(r - 2 * i + ndp, ndp)
        pltpu.make_async_remote_copy(
            src_ref=RA.at[:, rows_of(q)], dst_ref=RA.at[:, rows_of(q)],
            send_sem=rsend.at[i], recv_sem=rrecv.at[i],
            device_id=(s, q), device_id_type=MESH,
        ).wait_recv()

    def r_swap(rows):
        return pltpu.make_async_remote_copy(
            src_ref=RA.at[:, rows], dst_ref=RA.at[:, rows],
            send_sem=rsend.at[0], recv_sem=rrecv.at[0],
            device_id=(s, core), device_id_type=MESH,
        )

    own_x = pltpu.make_async_copy(XB.at[r], XS.at[:, mine], loc.at[0])

    def exchange_early():
        for i in range(1, ndp // 2):
            r_copy(i).start()
        own_x.start()
        for i in range(1, ndp):
            x_copy(i).start()
        for i in range(1, ndp // 2):
            r_wait(i)
        r_swap(plane).start()

    pl.when(s < last)(exchange_early)

    def chunk_copy(m, k):
        part = pl.ds(k * per, per)
        return pltpu.make_async_remote_copy(
            src_ref=NX.at[m, part], dst_ref=DY.at[m, part],
            send_sem=csend.at[m, k], recv_sem=crecv.at[m, k],
            device_id=(jnp.maximum(s - 1, 0), r), device_id_type=MESH,
        )

    def q_copy(m, i):
        q = peer(2 * i)
        return pltpu.make_async_remote_copy(
            src_ref=DQ.at[m, mine], dst_ref=DQ.at[m, mine],
            send_sem=qsend.at[m, i], recv_sem=qrecv.at[m, i],
            device_id=(s, q), device_id_type=MESH,
        )

    def q_wait(m, i):
        q = lax.rem(r - 2 * i + ndp, ndp)
        pltpu.make_async_remote_copy(
            src_ref=DQ.at[m, rows_of(q)], dst_ref=DQ.at[m, rows_of(q)],
            send_sem=qsend.at[m, i], recv_sem=qrecv.at[m, i],
            device_id=(s, q), device_id_type=MESH,
        ).wait_recv()

    def q_swap(m, rows):
        return pltpu.make_async_remote_copy(
            src_ref=DQ.at[m, rows], dst_ref=DQ.at[m, rows],
            send_sem=qsend.at[m, 0], recv_sem=qrecv.at[m, 0],
            device_id=(s, core), device_id_type=MESH,
        )

    def y_copy(m, i):
        q = peer(i)
        return pltpu.make_async_remote_copy(
            src_ref=DY.at[m, q], dst_ref=DS.at[m, mine],
            send_sem=ysend.at[m, i], recv_sem=yrecv.at[m, i],
            device_id=(s, q), device_id_type=MESH,
        )

    def y_wait(m, i):
        q = lax.rem(r - i + ndp, ndp)
        pltpu.make_async_remote_copy(
            src_ref=DY.at[m, q], dst_ref=DS.at[m, rows_of(q)],
            send_sem=ysend.at[m, i], recv_sem=yrecv.at[m, i],
            device_id=(s, q), device_id_type=MESH,
        ).wait_recv()

    @pl.when(s == last)
    def _():
        for i in range(ndp):
            pltpu.make_async_copy(
                out_grad.at[:, :, pl.ds(i * blk, blk)], DY.at[:, i], outsem.at[i]
            ).wait()

    def step(m, carry):
        d_mixed = jnp.zeros((tok, cols), F32)
        for k in range(nchunk):
            @pl.when(s < last)
            def _():
                chunk_copy(m, k).wait_recv()

            for j in range(k * per, (k + 1) * per):
                d_mixed += dot(DY[m, j], WO[j])
        d_mixed = d_mixed.astype(BF)
        parts = [[], [], []]
        for h in range(heads):
            q = QKV[m, :, h * hd : (h + 1) * hd]
            k = QKV[m, :, cols + h * hd : cols + (h + 1) * hd]
            v = QKV[m, :, 2 * cols + h * hd : 2 * cols + (h + 1) * hd]
            dr = d_mixed[:, h * hd : (h + 1) * hd]
            d_score = (dot_nt(dr, v) * TAB[h] / hd).astype(BF)
            parts[0].append(dot(d_score, k).astype(BF))
            parts[1].append(dot_tn(d_score, q).astype(BF))
            parts[2].append(dot_tn(SC[m, h], dr).astype(BF))
        d_all = jnp.concatenate(parts[0] + parts[1] + parts[2], axis=1)
        for k in range(nchunk):
            for j in range(k * per, (k + 1) * per):
                back = dot_nt(d_all, WI[j])
                NX[m, j] = (DY[m, j].astype(F32) + back).astype(BF)

            @pl.when(s > 0)
            def _():
                chunk_copy(m, k).start()

        DQ[m, mine] = (d_all.astype(F32) * live).astype(BF)
        for i in range(1, ndp // 2):
            q_copy(m, i).start()
        DS[m, mine] = DY[m, r]
        for i in range(1, ndp):
            y_copy(m, i).start()

        @pl.when(m > 0)
        def _():
            for i in range(1, ndp // 2):
                q_wait(m - 1, i)
            q_swap(m - 1, plane).start()

        return carry

    lax.fori_loop(0, micro, step, 0)
    write = pltpu.make_async_copy(NX, in_grad, outsem.at[0])
    write.start()

    pl.when(s == last)(exchange_early)

    for i in range(1, ndp):
        x_wait(i)
    own_x.wait()
    r_swap(foreign).wait_recv()
    scale = 1.0 / (ndp - 2 + 1.0)
    for m in range(micro - 1):
        q_swap(m, foreign).wait_recv()
        for i in range(1, ndp):
            y_wait(m, i)
        if m == 0:
            GI[...] = dot_tn(XS[m], DQ[m])
            GO[...] = dot_tn(DS[m], RA[m])
        else:
            GI[...] += dot_tn(XS[m], DQ[m])
            GO[...] += dot_tn(DS[m], RA[m])
    m = micro - 1
    for i in range(1, ndp // 2):
        q_wait(m, i)
    q_swap(m, plane).start()
    for i in range(1, ndp):
        y_wait(m, i)
    GO[...] = (GO[...] + dot_tn(DS[m], RA[m])) * scale
    out1 = pltpu.make_async_copy(GO, grad_out.at[0], outsem.at[1])
    out1.start()
    q_swap(m, foreign).wait_recv()
    GI[...] = (GI[...] + dot_tn(XS[m], DQ[m])) * scale
    out2 = pltpu.make_async_copy(GI, grad_in.at[0], outsem.at[2])
    out2.start()

    for copy in sent:
        copy.wait_send()
    for i in range(1, ndp):
        x_copy(i).wait_send()
    for i in range(1, ndp // 2):
        r_copy(i).wait_send()
    r_swap(plane).wait_send()

    def drain(m, carry):
        @pl.when(s > 0)
        def _():
            for k in range(nchunk):
                chunk_copy(m, k).wait_send()

        for i in range(1, ndp // 2):
            q_copy(m, i).wait_send()
        q_swap(m, plane).wait_send()
        for i in range(1, ndp):
            y_copy(m, i).wait_send()
        return carry

    lax.fori_loop(0, micro, drain, 0)
    write.wait()
    out1.wait()
    out2.wait()


def shards(acts, out_grad, w_in, w_out, decay_rate, cycle_order):
    nsec = lax.axis_size("section")
    ndp = lax.axis_size("dp")
    _, micro, tok, width = acts.shape
    cols = w_out.shape[2]
    heads = decay_rate.shape[1]
    hd = cols // heads
    blk = width // ndp
    nchunk = 4
    dims = (nsec, ndp, micro, tok, width, heads, hd, nchunk)
    dma = pltpu.SemaphoreType.DMA
    any_spec = pl.BlockSpec(memory_space=pl.ANY)
    smem = pl.BlockSpec(memory_space=pltpu.SMEM)
    in_grad, grad_in, grad_out = pl.pallas_call(
        functools.partial(kernel, dims),
        name="retention_stack_back",
        out_shape=(
            jax.ShapeDtypeStruct((micro, ndp, tok, blk), BF),
            jax.ShapeDtypeStruct((1, blk, 3 * cols), F32),
            jax.ShapeDtypeStruct((1, blk, cols), F32),
        ),
        in_specs=[any_spec] * 4 + [smem] * 2,
        out_specs=[any_spec] * 3,
        scratch_shapes=[
            pltpu.VMEM((ndp, blk, 3 * cols), BF),
            pltpu.VMEM((ndp, blk, cols), BF),
            pltpu.VMEM((ndp, micro, tok, blk), BF),
            pltpu.VMEM((micro, ndp, tok, blk), BF),
            pltpu.VMEM((micro, ndp, tok, blk), BF),
            pltpu.VMEM((micro * tok, 3 * cols), F32),
            pltpu.VMEM((micro, tok, 3 * cols), BF),
            pltpu.VMEM((micro, heads, tok, tok), BF),
            pltpu.VMEM((tok, cols), F32),
            pltpu.VMEM((heads, tok, tok), F32),
            pltpu.VMEM((micro, ndp * tok, blk), BF),
            pltpu.VMEM((micro, ndp * tok, blk), BF),
            pltpu.VMEM((micro, ndp * tok, 3 * cols), BF),
            pltpu.VMEM((micro, ndp * tok, cols), BF),
            pltpu.VMEM((blk, 3 * cols), F32),
            pltpu.VMEM((blk, cols), F32),
            dma((2 + ndp,)),
            dma((64,)),
            dma((ndp, 2, 2)),
            dma((micro, nchunk)),
            dma((micro, nchunk)),
            dma((ndp,)),
            dma((ndp,)),
            dma((ndp // 2,)),
            dma((ndp // 2,)),
            dma((micro, ndp // 2)),
            dma((micro, ndp // 2)),
            dma((micro, ndp)),
            dma((micro, ndp)),
            dma((ndp,)),
        ],
        compiler_params=pltpu.CompilerParams(
            collective_id=0, has_side_effects=True, vmem_limit_bytes=60 * 1024 * 1024
        ),
        cost_estimate=pl.CostEstimate(
            flops=6_000_000_000, bytes_accessed=8_000_000, transcendentals=4096
        ),
    )(acts, out_grad, w_in, w_out, decay_rate, cycle_order)
    in_grad = jnp.swapaxes(in_grad, 1, 2).reshape(1, micro, tok, width)
    return (in_grad, grad_in, grad_out)


def solution(mesh):
    placed = (
        P("section", None, "dp", None),
        P(None, "dp", None),
        P("section", "dp", None),
        P("section", "dp", None),
        P("section", None),
        P(),
    )
    return jax.shard_map(
        shards,
        mesh=mesh,
        in_specs=placed,
        out_specs=(
            P("section", None, "dp", None),
            P("section", "dp", None),
            P("section", "dp", None),
        ),
        check_vma=False,
    )
```

```python
import functools

import jax
import jax.numpy as jnp
from jax import lax
from jax.experimental import pallas as pl
from jax.experimental.pallas import tpu as pltpu
from jax.sharding import PartitionSpec as P

MESH = pl.DeviceIdType.MESH
BF = jnp.bfloat16
F32 = jnp.float32


def dot(a, b):
    return jnp.dot(a, b, preferred_element_type=F32)


def dot_nt(a, b):
    return lax.dot_general(a, b, (((1,), (1,)), ((), ())), preferred_element_type=F32)


def dot_tn(a, b):
    return lax.dot_general(a, b, (((0,), (0,)), ((), ())), preferred_element_type=F32)


def kernel(
    dims,
    acts, out_grad, w_in, w_out, rates, order,
    in_grad, grad_in, grad_out,
    WI, WO, WT, XB, DY, NX, ACC, QKV, SC, TAB, XS, DS, DQ, RA, GI, GO,
    loc, wsend, wrecv, csend, crecv, xsend, xrecv, rsend, rrecv, qsend, qrecv, ysend, yrecv, outsem,
):
    nsec, ndp, micro, tok, width, heads, hd, nchunk = dims
    cols = heads * hd
    blk = width // ndp
    half = blk // 2
    per = ndp // nchunk
    nx = ndp // 4
    s = lax.axis_index("section")
    r = lax.axis_index("dp")
    x, zl, c = r // 4, (r // 2) % 2, r % 2
    last = nsec - 1
    lead = min(4, nsec // 4)
    slot = c * (ndp // 2) + r // 2

    def rep(xx, zz, cc):
        return lax.rem(xx + nx, nx) * 4 + zz * 2 + cc

    core, zp = rep(x, zl, 1 - c), rep(x, 1 - zl, c)
    xp, xm, xo = rep(x + 1, zl, c), rep(x - 1, zl, c), rep(x + 2, zl, c)
    xpz, xmz, xoz = rep(x + 1, 1 - zl, c), rep(x - 1, 1 - zl, c), rep(x + 2, 1 - zl, c)

    def peer(i):
        return lax.rem(r + i, ndp)

    def slot_of(q):
        return lax.rem(q, 2) * (ndp // 2) + q // 2

    local = [
        pltpu.make_async_copy(w_in.at[0], WI.at[r], loc.at[0]),
        pltpu.make_async_copy(w_out.at[0], WO.at[r], loc.at[1]),
    ]
    for i in range(ndp):
        local.append(
            pltpu.make_async_copy(
                acts.at[0, :, :, pl.ds(i * blk, blk)], XB.at[i], loc.at[2 + i]
            )
        )
    for copy in local:
        copy.start()

    barrier = pltpu.get_barrier_semaphore()
    for i in range(1, ndp):
        pl.semaphore_signal(barrier, inc=1, device_id=(s, peer(i)), device_id_type=MESH)

    @pl.when(s > 0)
    def _():
        pl.semaphore_signal(barrier, inc=1, device_id=(s - 1, r), device_id_type=MESH)

    @pl.when(s < last)
    def _():
        pl.semaphore_signal(barrier, inc=1, device_id=(s + 1, r), device_id_type=MESH)

    neighbours = jnp.where(s > 0, 1, 0) + jnp.where(s < last, 1, 0)
    pl.semaphore_wait(barrier, ndp - 1 + neighbours)

    def piece(ref, q, h):
        return ref.at[q, pl.ds(h * half, half)]

    sent = []

    def push(q, h, target, own=False):
        for which, ref in enumerate((WI, WO)):
            if own:
                src = (w_in, w_out)[which].at[0, pl.ds(h * half, half)]
            else:
                src = piece(ref, q, h)
            copy = pltpu.make_async_remote_copy(
                src_ref=src,
                dst_ref=piece(ref, q, h),
                send_sem=wsend.at[len(sent)],
                recv_sem=wrecv.at[q, h, which],
                device_id=(s, target),
                device_id_type=MESH,
            )
            copy.start()
            sent.append(copy)

    def arrive(q, h):
        for which, ref in enumerate((WI, WO)):
            pltpu.make_async_remote_copy(
                src_ref=piece(ref, q, h),
                dst_ref=piece(ref, q, h),
                send_sem=wsend.at[0],
                recv_sem=wrecv.at[q, h, which],
                device_id=(s, core),
                device_id_type=MESH,
            ).wait_recv()

    for h in range(2):
        for target in (xp, xm, zp, core):
            push(r, h, target, own=True)

    ACC[...] = jnp.zeros_like(ACC)

    def add(q):
        ACC[...] += dot(XB[q].reshape(micro * tok, blk), WI[q])
        WT[q] = WI[q].T

    for copy in local:
        copy.wait()

    @pl.when(s == last)
    def _():
        for i in range(ndp):
            pltpu.make_async_copy(
                out_grad.at[:, :, pl.ds(i * blk, blk)], DY.at[:, i], outsem.at[i]
            ).start()

    spot_t = lax.broadcasted_iota(jnp.int32, (tok, tok), 0)
    spot_j = lax.broadcasted_iota(jnp.int32, (tok, tok), 1)
    offset = (spot_t - spot_j).astype(F32)
    for h in range(heads):
        decayed = jnp.exp(-rates[0, h] * jnp.maximum(offset, 0.0))
        TAB[h] = jnp.where(offset >= 0.0, decayed, 0.0)

    add(r)
    arrive(xm, 0)
    push(xm, 0, xp)
    push(xm, 0, core)
    arrive(xp, 0)
    push(xp, 0, core)
    arrive(zp, 0)
    push(zp, 0, xp)
    push(zp, 0, xm)
    push(zp, 0, core)
    arrive(core, 0)
    arrive(core, 1)
    add(core)
    arrive(xp, 1)
    push(xp, 1, xm)
    push(xp, 1, core)
    arrive(xm, 1)
    push(xm, 1, core)
    arrive(zp, 1)
    push(zp, 1, xp)
    push(zp, 1, xm)
    push(zp, 1, core)
    add(xm)
    add(xp)
    add(zp)
    arrive(xo, 0)
    push(xo, 0, zp)
    push(xo, 0, core)
    arrive(xo, 1)
    push(xo, 1, zp)
    push(xo, 1, core)

    def other(q):
        return q + 1 - 2 * c

    for q in (xm, xp, zp):
        arrive(other(q), 0)
        arrive(other(q), 1)
        add(other(q))
    add(xo)
    for q in (xmz, xpz):
        for h in range(2):
            arrive(q, h)
            push(q, h, core)
    arrive(xoz, 0)
    push(xoz, 0, core)
    add(xmz)
    add(xpz)
    arrive(xoz, 1)
    push(xoz, 1, core)
    for q in (xo, xmz, xpz):
        arrive(other(q), 0)
        arrive(other(q), 1)
        add(other(q))
    add(xoz)
    arrive(other(xoz), 0)
    arrive(other(xoz), 1)
    add(other(xoz))

    failed = order[ndp - 1]
    live = jnp.where(r == failed, 0.0, 1.0).astype(F32)
    mine = pl.ds(pl.multiple_of(slot * tok, tok), tok)

    QKV[...] = ACC[...].astype(BF).reshape(micro, tok, 3 * cols)
    for m in range(micro):
        for h in range(heads):
            q = QKV[m, :, h * hd : (h + 1) * hd]
            k = QKV[m, :, cols + h * hd : cols + (h + 1) * hd]
            v = QKV[m, :, 2 * cols + h * hd : 2 * cols + (h + 1) * hd]
            score = (dot_nt(q, k) * TAB[h] / hd).astype(BF)
            SC[m, h] = score
            mixed = dot(score, v).astype(BF)
            RA[m, mine, h * hd : (h + 1) * hd] = (mixed.astype(F32) * live).astype(BF)

    plane = pl.ds(pl.multiple_of(c * (ndp // 2) * tok, tok), (ndp // 2) * tok)
    foreign = pl.ds(pl.multiple_of((1 - c) * (ndp // 2) * tok, tok), (ndp // 2) * tok)

    def rows_of(q):
        return pl.ds(pl.multiple_of(slot_of(q) * tok, tok), tok)

    def x_copy(i):
        q = peer(i)
        return pltpu.make_async_remote_copy(
            src_ref=XB.at[q], dst_ref=XS.at[:, mine],
            send_sem=xsend.at[i], recv_sem=xrecv.at[i],
            device_id=(s, q), device_id_type=MESH,
        )

    def x_wait(i):
        q = lax.rem(r - i + ndp, ndp)
        pltpu.make_async_remote_copy(
            src_ref=XB.at[q], dst_ref=XS.at[:, rows_of(q)],
            send_sem=xsend.at[i], recv_sem=xrecv.at[i],
            device_id=(s, q), device_id_type=MESH,
        ).wait_recv()

    def r_copy(i):
        q = peer(2 * i)
        return pltpu.make_async_remote_copy(
            src_ref=RA.at[:, mine], dst_ref=RA.at[:, mine],
            send_sem=rsend.at[i], recv_sem=rrecv.at[i],
            device_id=(s, q), device_id_type=MESH,
        )

    def r_wait(i):
        q = lax.rem(r - 2 * i + ndp, ndp)
        pltpu.make_async_remote_copy(
            src_ref=RA.at[:, rows_of(q)], dst_ref=RA.at[:, rows_of(q)],
            send_sem=rsend.at[i], recv_sem=rrecv.at[i],
            device_id=(s, q), device_id_type=MESH,
        ).wait_recv()

    def r_swap(rows):
        return pltpu.make_async_remote_copy(
            src_ref=RA.at[:, rows], dst_ref=RA.at[:, rows],
            send_sem=rsend.at[0], recv_sem=rrecv.at[0],
            device_id=(s, core), device_id_type=MESH,
        )

    own_x = pltpu.make_async_copy(XB.at[r], XS.at[:, mine], loc.at[0])

    def exchange_early():
        for i in range(1, ndp // 2):
            r_copy(i).start()
        own_x.start()
        for i in range(1, ndp):
            x_copy(i).start()
        for i in range(1, ndp // 2):
            r_wait(i)
        r_swap(plane).start()
        own_x.wait()
        for i in range(1, ndp):
            x_wait(i)
        r_swap(foreign).wait_recv()

    GI[...] = jnp.zeros_like(GI)
    GO[...] = jnp.zeros_like(GO)
    early = s < last - lead
    pl.when(early)(exchange_early)

    def chunk_copy(m, k):
        part = pl.ds(k * per, per)
        return pltpu.make_async_remote_copy(
            src_ref=NX.at[m, part], dst_ref=DY.at[m, part],
            send_sem=csend.at[m, k], recv_sem=crecv.at[m, k],
            device_id=(jnp.maximum(s - 1, 0), r), device_id_type=MESH,
        )

    def q_copy(m, i):
        q = peer(2 * i)
        return pltpu.make_async_remote_copy(
            src_ref=DQ.at[m, mine], dst_ref=DQ.at[m, mine],
            send_sem=qsend.at[m, i], recv_sem=qrecv.at[m, i],
            device_id=(s, q), device_id_type=MESH,
        )

    def q_wait(m, i):
        q = lax.rem(r - 2 * i + ndp, ndp)
        pltpu.make_async_remote_copy(
            src_ref=DQ.at[m, rows_of(q)], dst_ref=DQ.at[m, rows_of(q)],
            send_sem=qsend.at[m, i], recv_sem=qrecv.at[m, i],
            device_id=(s, q), device_id_type=MESH,
        ).wait_recv()

    def q_swap(m, rows):
        return pltpu.make_async_remote_copy(
            src_ref=DQ.at[m, rows], dst_ref=DQ.at[m, rows],
            send_sem=qsend.at[m, 0], recv_sem=qrecv.at[m, 0],
            device_id=(s, core), device_id_type=MESH,
        )

    def y_copy(m, i):
        q = peer(i)
        return pltpu.make_async_remote_copy(
            src_ref=DY.at[m, q], dst_ref=DS.at[m, mine],
            send_sem=ysend.at[m, i], recv_sem=yrecv.at[m, i],
            device_id=(s, q), device_id_type=MESH,
        )

    def y_wait(m, i):
        q = lax.rem(r - i + ndp, ndp)
        pltpu.make_async_remote_copy(
            src_ref=DY.at[m, q], dst_ref=DS.at[m, rows_of(q)],
            send_sem=ysend.at[m, i], recv_sem=yrecv.at[m, i],
            device_id=(s, q), device_id_type=MESH,
        ).wait_recv()

    @pl.when(s == last)
    def _():
        for i in range(ndp):
            pltpu.make_async_copy(
                out_grad.at[:, :, pl.ds(i * blk, blk)], DY.at[:, i], outsem.at[i]
            ).wait()

    def settle(m):
        q_swap(m, foreign).wait_recv()
        for i in range(1, ndp):
            y_wait(m, i)
        GI[...] += dot_tn(XS[m], DQ[m])
        GO[...] += dot_tn(DS[m], RA[m])

    def step(m, carry):
        d_mixed = jnp.zeros((tok, cols), F32)
        for k in range(nchunk):
            @pl.when(s < last)
            def _():
                chunk_copy(m, k).wait_recv()

            for j in range(k * per, (k + 1) * per):
                d_mixed += dot(DY[m, j], WO[j])
        d_mixed = d_mixed.astype(BF)
        parts = [[], [], []]
        for h in range(heads):
            q = QKV[m, :, h * hd : (h + 1) * hd]
            k = QKV[m, :, cols + h * hd : cols + (h + 1) * hd]
            v = QKV[m, :, 2 * cols + h * hd : 2 * cols + (h + 1) * hd]
            dr = d_mixed[:, h * hd : (h + 1) * hd]
            d_score = (dot_nt(dr, v) * TAB[h] / hd).astype(BF)
            parts[0].append(dot(d_score, k).astype(BF))
            parts[1].append(dot_tn(d_score, q).astype(BF))
            parts[2].append(dot_tn(SC[m, h], dr).astype(BF))
        d_all = jnp.concatenate(parts[0] + parts[1] + parts[2], axis=1)
        for k in range(nchunk):
            for j in range(k * per, (k + 1) * per):
                back = dot(d_all, WT[j])
                NX[m, j] = (DY[m, j].astype(F32) + back).astype(BF)

            @pl.when(s > 0)
            def _():
                chunk_copy(m, k).start()

        DQ[m, mine] = (d_all.astype(F32) * live).astype(BF)
        for i in range(1, ndp // 2):
            q_copy(m, i).start()
        DS[m, mine] = DY[m, r]
        for i in range(1, ndp):
            y_copy(m, i).start()

        @pl.when(m > 0)
        def _():
            for i in range(1, ndp // 2):
                q_wait(m - 1, i)
            q_swap(m - 1, plane).start()

        @pl.when((m > 1) & early)
        def _():
            settle(m - 2)

        return carry

    lax.fori_loop(0, micro, step, 0)
    writes = [
        pltpu.make_async_copy(
            NX.at[:, i], in_grad.at[0, :, :, pl.ds(i * blk, blk)], outsem.at[i]
        )
        for i in range(ndp)
    ]
    for copy in writes:
        copy.start()

    pl.when(s >= last - lead)(exchange_early)

    scale = 1.0 / (ndp - 1.0)

    @pl.when(s >= last - lead)
    def _():
        for m in range(micro - 2):
            settle(m)

    settle(micro - 2)
    m = micro - 1
    for i in range(1, ndp // 2):
        q_wait(m, i)
    q_swap(m, plane).start()
    for i in range(1, ndp):
        y_wait(m, i)
    GO[...] = (GO[...] + dot_tn(DS[m], RA[m])) * scale
    out1 = pltpu.make_async_copy(GO, grad_out.at[0], loc.at[1])
    out1.start()
    q_swap(m, foreign).wait_recv()
    GI[...] = (GI[...] + dot_tn(XS[m], DQ[m])) * scale
    out2 = pltpu.make_async_copy(GI, grad_in.at[0], loc.at[2])
    out2.start()

    for copy in sent:
        copy.wait_send()
    for i in range(1, ndp):
        x_copy(i).wait_send()
    for i in range(1, ndp // 2):
        r_copy(i).wait_send()
    r_swap(plane).wait_send()

    def drain(m, carry):
        @pl.when(s > 0)
        def _():
            for k in range(nchunk):
                chunk_copy(m, k).wait_send()

        for i in range(1, ndp // 2):
            q_copy(m, i).wait_send()
        q_swap(m, plane).wait_send()
        for i in range(1, ndp):
            y_copy(m, i).wait_send()
        return carry

    lax.fori_loop(0, micro, drain, 0)
    for copy in writes:
        copy.wait()
    out1.wait()
    out2.wait()


def shards(acts, out_grad, w_in, w_out, decay_rate, cycle_order):
    nsec = lax.axis_size("section")
    ndp = lax.axis_size("dp")
    _, micro, tok, width = acts.shape
    cols = w_out.shape[2]
    heads = decay_rate.shape[1]
    hd = cols // heads
    blk = width // ndp
    nchunk = 4
    dims = (nsec, ndp, micro, tok, width, heads, hd, nchunk)
    dma = pltpu.SemaphoreType.DMA
    any_spec = pl.BlockSpec(memory_space=pl.ANY)
    smem = pl.BlockSpec(memory_space=pltpu.SMEM)
    return pl.pallas_call(
        functools.partial(kernel, dims),
        name="retention_stack_back",
        out_shape=(
            jax.ShapeDtypeStruct((1, micro, tok, width), BF),
            jax.ShapeDtypeStruct((1, blk, 3 * cols), F32),
            jax.ShapeDtypeStruct((1, blk, cols), F32),
        ),
        in_specs=[any_spec] * 4 + [smem] * 2,
        out_specs=[any_spec] * 3,
        scratch_shapes=[
            pltpu.VMEM((ndp, blk, 3 * cols), BF),
            pltpu.VMEM((ndp, blk, cols), BF),
            pltpu.VMEM((ndp, 3 * cols, blk), BF),
            pltpu.VMEM((ndp, micro, tok, blk), BF),
            pltpu.VMEM((micro, ndp, tok, blk), BF),
            pltpu.VMEM((micro, ndp, tok, blk), BF),
            pltpu.VMEM((micro * tok, 3 * cols), F32),
            pltpu.VMEM((micro, tok, 3 * cols), BF),
            pltpu.VMEM((micro, heads, tok, tok), BF),
            pltpu.VMEM((heads, tok, tok), F32),
            pltpu.VMEM((micro, ndp * tok, blk), BF),
            pltpu.VMEM((micro, ndp * tok, blk), BF),
            pltpu.VMEM((micro, ndp * tok, 3 * cols), BF),
            pltpu.VMEM((micro, ndp * tok, cols), BF),
            pltpu.VMEM((blk, 3 * cols), F32),
            pltpu.VMEM((blk, cols), F32),
            dma((2 + ndp,)),
            dma((64,)),
            dma((ndp, 2, 2)),
            dma((micro, nchunk)),
            dma((micro, nchunk)),
            dma((ndp,)),
            dma((ndp,)),
            dma((ndp // 2,)),
            dma((ndp // 2,)),
            dma((micro, ndp // 2)),
            dma((micro, ndp // 2)),
            dma((micro, ndp)),
            dma((micro, ndp)),
            dma((ndp,)),
        ],
        compiler_params=pltpu.CompilerParams(
            collective_id=0, has_side_effects=True, vmem_limit_bytes=60 * 1024 * 1024
        ),
        cost_estimate=pl.CostEstimate(
            flops=6_000_000_000, bytes_accessed=8_000_000, transcendentals=4096
        ),
    )(acts, out_grad, w_in, w_out, decay_rate, cycle_order)


def solution(mesh):
    placed = (
        P("section", None, "dp", None),
        P(None, "dp", None),
        P("section", "dp", None),
        P("section", "dp", None),
        P("section", None),
        P(),
    )
    return jax.shard_map(
        shards,
        mesh=mesh,
        in_specs=placed,
        out_specs=(
            P("section", None, "dp", None),
            P("section", "dp", None),
            P("section", "dp", None),
        ),
        check_vma=False,
    )
```

```python
import functools

import jax
import jax.numpy as jnp
from jax import lax
from jax.experimental import pallas as pl
from jax.experimental.pallas import tpu as pltpu
from jax.sharding import PartitionSpec as P

MESH = pl.DeviceIdType.MESH
BF = jnp.bfloat16
F32 = jnp.float32


def dot(a, b):
    return jnp.dot(a, b, preferred_element_type=F32)


def dot_nt(a, b):
    return lax.dot_general(a, b, (((1,), (1,)), ((), ())), preferred_element_type=F32)


def dot_tn(a, b):
    return lax.dot_general(a, b, (((0,), (0,)), ((), ())), preferred_element_type=F32)


def kernel(
    dims,
    acts, out_grad, w_in, w_out, rates, order,
    in_grad, grad_in, grad_out,
    WI, WO, WT, XB, DY, NX, RB, ACC, QKV, SC, TAB, XS, DS, DQ, RA, GI, GO,
    loc, wsend, wrecv, csend, crecv, bsend, brecv, xsend, xrecv, rsend, rrecv, qsend, qrecv, ysend, yrecv, outsem,
):
    nsec, ndp, micro, tok, width, heads, hd, nchunk = dims
    cols = heads * hd
    blk = width // ndp
    half = blk // 2
    per = ndp // nchunk
    nx = ndp // 4
    s = lax.axis_index("section")
    r = lax.axis_index("dp")
    x, zl, c = r // 4, (r // 2) % 2, r % 2
    last = nsec - 1
    lead = min(4, nsec // 4)
    ny = 4 if nsec >= 16 else 2
    y = lax.rem(s, ny)
    to_relay = (s > 0) & (y == 0) & (zl == 0)
    to_next = (s > 0) & ((y != 0) | (zl != 0))
    node = (s >= ny) & (y == ny - 1) & (zl == 0)
    by_relay = (s < last) & (y == ny - 1) & (zl == 0)
    by_prev = (s < last) & ((y != ny - 1) | (zl != 0))
    slot = c * (ndp // 2) + r // 2

    def rep(xx, zz, cc):
        return lax.rem(xx + nx, nx) * 4 + zz * 2 + cc

    core, zp = rep(x, zl, 1 - c), rep(x, 1 - zl, c)
    xp, xm, xo = rep(x + 1, zl, c), rep(x - 1, zl, c), rep(x + 2, zl, c)
    xpz, xmz, xoz = rep(x + 1, 1 - zl, c), rep(x - 1, 1 - zl, c), rep(x + 2, 1 - zl, c)

    def peer(i):
        return lax.rem(r + i, ndp)

    def slot_of(q):
        return lax.rem(q, 2) * (ndp // 2) + q // 2

    local = [
        pltpu.make_async_copy(w_in.at[0], WI.at[r], loc.at[0]),
        pltpu.make_async_copy(w_out.at[0], WO.at[r], loc.at[1]),
    ]
    for i in range(ndp):
        local.append(
            pltpu.make_async_copy(
                acts.at[0, :, :, pl.ds(i * blk, blk)], XB.at[i], loc.at[2 + i]
            )
        )
    for copy in local:
        copy.start()

    barrier = pltpu.get_barrier_semaphore()
    for i in range(1, ndp):
        pl.semaphore_signal(barrier, inc=1, device_id=(s, peer(i)), device_id_type=MESH)

    def greet(cond, section):
        @pl.when(cond)
        def _():
            pl.semaphore_signal(
                barrier, inc=1, device_id=(section, r), device_id_type=MESH
            )

    greet(by_prev, jnp.minimum(s + 1, last))
    greet(by_relay, jnp.minimum(s + ny, last))
    greet(node, jnp.maximum(s - (ny - 1), 0))
    receivers = (
        jnp.where(to_next, 1, 0) + jnp.where(to_relay, 1, 0) + jnp.where(node, 1, 0)
    )
    pl.semaphore_wait(barrier, ndp - 1 + receivers)

    def piece(ref, q, h):
        return ref.at[q, pl.ds(h * half, half)]

    sent = []

    def push(q, h, target, own=False):
        for which, ref in enumerate((WI, WO)):
            if own:
                src = (w_in, w_out)[which].at[0, pl.ds(h * half, half)]
            else:
                src = piece(ref, q, h)
            copy = pltpu.make_async_remote_copy(
                src_ref=src,
                dst_ref=piece(ref, q, h),
                send_sem=wsend.at[len(sent)],
                recv_sem=wrecv.at[q, h, which],
                device_id=(s, target),
                device_id_type=MESH,
            )
            copy.start()
            sent.append(copy)

    def arrive(q, h):
        for which, ref in enumerate((WI, WO)):
            pltpu.make_async_remote_copy(
                src_ref=piece(ref, q, h),
                dst_ref=piece(ref, q, h),
                send_sem=wsend.at[0],
                recv_sem=wrecv.at[q, h, which],
                device_id=(s, core),
                device_id_type=MESH,
            ).wait_recv()

    for h in range(2):
        for target in (xp, xm, zp, core):
            push(r, h, target, own=True)

    ACC[...] = jnp.zeros_like(ACC)

    def add(q):
        ACC[...] += dot(XB[q].reshape(micro * tok, blk), WI[q])
        WT[q] = WI[q].T

    for copy in local:
        copy.wait()

    @pl.when(s == last)
    def _():
        for i in range(ndp):
            pltpu.make_async_copy(
                out_grad.at[:, :, pl.ds(i * blk, blk)], DY.at[:, i], outsem.at[i]
            ).start()

    spot_t = lax.broadcasted_iota(jnp.int32, (tok, tok), 0)
    spot_j = lax.broadcasted_iota(jnp.int32, (tok, tok), 1)
    offset = (spot_t - spot_j).astype(F32)
    for h in range(heads):
        decayed = jnp.exp(-rates[0, h] * jnp.maximum(offset, 0.0))
        TAB[h] = jnp.where(offset >= 0.0, decayed, 0.0)

    add(r)
    arrive(xm, 0)
    push(xm, 0, xp)
    push(xm, 0, core)
    arrive(xp, 0)
    push(xp, 0, core)
    arrive(zp, 0)
    push(zp, 0, xp)
    push(zp, 0, xm)
    push(zp, 0, core)
    arrive(core, 0)
    arrive(core, 1)
    add(core)
    arrive(xp, 1)
    push(xp, 1, xm)
    push(xp, 1, core)
    arrive(xm, 1)
    push(xm, 1, core)
    arrive(zp, 1)
    push(zp, 1, xp)
    push(zp, 1, xm)
    push(zp, 1, core)
    add(xm)
    add(xp)
    add(zp)
    arrive(xo, 0)
    push(xo, 0, zp)
    push(xo, 0, core)
    arrive(xo, 1)
    push(xo, 1, zp)
    push(xo, 1, core)

    def other(q):
        return q + 1 - 2 * c

    for q in (xm, xp, zp):
        arrive(other(q), 0)
        arrive(other(q), 1)
        add(other(q))
    add(xo)
    for q in (xmz, xpz):
        for h in range(2):
            arrive(q, h)
            push(q, h, core)
    arrive(xoz, 0)
    push(xoz, 0, core)
    add(xmz)
    add(xpz)
    arrive(xoz, 1)
    push(xoz, 1, core)
    for q in (xo, xmz, xpz):
        arrive(other(q), 0)
        arrive(other(q), 1)
        add(other(q))
    add(xoz)
    arrive(other(xoz), 0)
    arrive(other(xoz), 1)
    add(other(xoz))

    failed = order[ndp - 1]
    live = jnp.where(r == failed, 0.0, 1.0).astype(F32)
    mine = pl.ds(pl.multiple_of(slot * tok, tok), tok)

    QKV[...] = ACC[...].astype(BF).reshape(micro, tok, 3 * cols)
    for m in range(micro):
        for h in range(heads):
            q = QKV[m, :, h * hd : (h + 1) * hd]
            k = QKV[m, :, cols + h * hd : cols + (h + 1) * hd]
            v = QKV[m, :, 2 * cols + h * hd : 2 * cols + (h + 1) * hd]
            score = (dot_nt(q, k) * TAB[h] / hd).astype(BF)
            SC[m, h] = score
            mixed = dot(score, v).astype(BF)
            RA[m, mine, h * hd : (h + 1) * hd] = (mixed.astype(F32) * live).astype(BF)

    plane = pl.ds(pl.multiple_of(c * (ndp // 2) * tok, tok), (ndp // 2) * tok)
    foreign = pl.ds(pl.multiple_of((1 - c) * (ndp // 2) * tok, tok), (ndp // 2) * tok)

    def rows_of(q):
        return pl.ds(pl.multiple_of(slot_of(q) * tok, tok), tok)

    def x_copy(i):
        q = peer(i)
        return pltpu.make_async_remote_copy(
            src_ref=XB.at[q], dst_ref=XS.at[:, mine],
            send_sem=xsend.at[i], recv_sem=xrecv.at[i],
            device_id=(s, q), device_id_type=MESH,
        )

    def x_wait(i):
        q = lax.rem(r - i + ndp, ndp)
        pltpu.make_async_remote_copy(
            src_ref=XB.at[q], dst_ref=XS.at[:, rows_of(q)],
            send_sem=xsend.at[i], recv_sem=xrecv.at[i],
            device_id=(s, q), device_id_type=MESH,
        ).wait_recv()

    def r_copy(i):
        q = peer(2 * i)
        return pltpu.make_async_remote_copy(
            src_ref=RA.at[:, mine], dst_ref=RA.at[:, mine],
            send_sem=rsend.at[i], recv_sem=rrecv.at[i],
            device_id=(s, q), device_id_type=MESH,
        )

    def r_wait(i):
        q = lax.rem(r - 2 * i + ndp, ndp)
        pltpu.make_async_remote_copy(
            src_ref=RA.at[:, rows_of(q)], dst_ref=RA.at[:, rows_of(q)],
            send_sem=rsend.at[i], recv_sem=rrecv.at[i],
            device_id=(s, q), device_id_type=MESH,
        ).wait_recv()

    def r_swap(rows):
        return pltpu.make_async_remote_copy(
            src_ref=RA.at[:, rows], dst_ref=RA.at[:, rows],
            send_sem=rsend.at[0], recv_sem=rrecv.at[0],
            device_id=(s, core), device_id_type=MESH,
        )

    own_x = pltpu.make_async_copy(XB.at[r], XS.at[:, mine], loc.at[0])

    def exchange_early():
        for i in range(1, ndp // 2):
            r_copy(i).start()
        own_x.start()
        for i in range(1, ndp):
            x_copy(i).start()
        for i in range(1, ndp // 2):
            r_wait(i)
        r_swap(plane).start()
        own_x.wait()
        for i in range(1, ndp):
            x_wait(i)
        r_swap(foreign).wait_recv()

    GI[...] = jnp.zeros_like(GI)
    GO[...] = jnp.zeros_like(GO)
    early = s < last - lead
    pl.when(early)(exchange_early)

    def chunk_copy(m, k):
        part = pl.ds(k * per, per)
        return pltpu.make_async_remote_copy(
            src_ref=NX.at[m, part], dst_ref=DY.at[m, part],
            send_sem=csend.at[m, k], recv_sem=crecv.at[m, k],
            device_id=(jnp.maximum(s - 1, 0), r), device_id_type=MESH,
        )

    def relay_copy(m, k):
        part = pl.ds(k * per, per)
        return pltpu.make_async_remote_copy(
            src_ref=NX.at[m, part], dst_ref=RB.at[m, part],
            send_sem=csend.at[m, k], recv_sem=brecv.at[m, k],
            device_id=(jnp.minimum(s + ny - 1, last), r), device_id_type=MESH,
        )

    def pass_on(m, k):
        part = pl.ds(k * per, per)
        return pltpu.make_async_remote_copy(
            src_ref=RB.at[m, part], dst_ref=DY.at[m, part],
            send_sem=bsend.at[m, k], recv_sem=crecv.at[m, k],
            device_id=(jnp.maximum(s - ny, 0), r), device_id_type=MESH,
        )

    def q_copy(m, i):
        q = peer(2 * i)
        return pltpu.make_async_remote_copy(
            src_ref=DQ.at[m, mine], dst_ref=DQ.at[m, mine],
            send_sem=qsend.at[m, i], recv_sem=qrecv.at[m, i],
            device_id=(s, q), device_id_type=MESH,
        )

    def q_wait(m, i):
        q = lax.rem(r - 2 * i + ndp, ndp)
        pltpu.make_async_remote_copy(
            src_ref=DQ.at[m, rows_of(q)], dst_ref=DQ.at[m, rows_of(q)],
            send_sem=qsend.at[m, i], recv_sem=qrecv.at[m, i],
            device_id=(s, q), device_id_type=MESH,
        ).wait_recv()

    def q_swap(m, rows):
        return pltpu.make_async_remote_copy(
            src_ref=DQ.at[m, rows], dst_ref=DQ.at[m, rows],
            send_sem=qsend.at[m, 0], recv_sem=qrecv.at[m, 0],
            device_id=(s, core), device_id_type=MESH,
        )

    def y_copy(m, i):
        q = peer(i)
        return pltpu.make_async_remote_copy(
            src_ref=DY.at[m, q], dst_ref=DS.at[m, mine],
            send_sem=ysend.at[m, i], recv_sem=yrecv.at[m, i],
            device_id=(s, q), device_id_type=MESH,
        )

    def y_wait(m, i):
        q = lax.rem(r - i + ndp, ndp)
        pltpu.make_async_remote_copy(
            src_ref=DY.at[m, q], dst_ref=DS.at[m, rows_of(q)],
            send_sem=ysend.at[m, i], recv_sem=yrecv.at[m, i],
            device_id=(s, q), device_id_type=MESH,
        ).wait_recv()

    @pl.when(s == last)
    def _():
        for i in range(ndp):
            pltpu.make_async_copy(
                out_grad.at[:, :, pl.ds(i * blk, blk)], DY.at[:, i], outsem.at[i]
            ).wait()

    def settle(m):
        q_swap(m, foreign).wait_recv()
        for i in range(1, ndp):
            y_wait(m, i)
        GI[...] += dot_tn(XS[m], DQ[m])
        GO[...] += dot_tn(DS[m], RA[m])

    def step(m, carry):
        d_mixed = jnp.zeros((tok, cols), F32)
        for k in range(nchunk):
            @pl.when(s < last)
            def _():
                chunk_copy(m, k).wait_recv()

            for j in range(k * per, (k + 1) * per):
                d_mixed += dot(DY[m, j], WO[j])
        d_mixed = d_mixed.astype(BF)
        parts = [[], [], []]
        for h in range(heads):
            q = QKV[m, :, h * hd : (h + 1) * hd]
            k = QKV[m, :, cols + h * hd : cols + (h + 1) * hd]
            v = QKV[m, :, 2 * cols + h * hd : 2 * cols + (h + 1) * hd]
            dr = d_mixed[:, h * hd : (h + 1) * hd]
            d_score = (dot_nt(dr, v) * TAB[h] / hd).astype(BF)
            parts[0].append(dot(d_score, k).astype(BF))
            parts[1].append(dot_tn(d_score, q).astype(BF))
            parts[2].append(dot_tn(SC[m, h], dr).astype(BF))
        d_all = jnp.concatenate(parts[0] + parts[1] + parts[2], axis=1)
        for k in range(nchunk):
            for j in range(k * per, (k + 1) * per):
                back = dot(d_all, WT[j])
                NX[m, j] = (DY[m, j].astype(F32) + back).astype(BF)

            @pl.when(to_next)
            def _():
                chunk_copy(m, k).start()

            @pl.when(to_relay)
            def _():
                relay_copy(m, k).start()

        DQ[m, mine] = (d_all.astype(F32) * live).astype(BF)
        for i in range(1, ndp // 2):
            q_copy(m, i).start()
        DS[m, mine] = DY[m, r]
        for i in range(1, ndp):
            y_copy(m, i).start()

        @pl.when(m > 0)
        def _():
            for i in range(1, ndp // 2):
                q_wait(m - 1, i)
            q_swap(m - 1, plane).start()

        @pl.when((m > 1) & early)
        def _():
            settle(m - 2)

        return carry

    lax.fori_loop(0, micro, step, 0)
    writes = [
        pltpu.make_async_copy(
            NX.at[:, i], in_grad.at[0, :, :, pl.ds(i * blk, blk)], outsem.at[i]
        )
        for i in range(ndp)
    ]
    for copy in writes:
        copy.start()

    @pl.when(node)
    def _():
        def forward(m, carry):
            for k in range(nchunk):
                relay_copy(m, k).wait_recv()
                pass_on(m, k).start()
            return carry

        lax.fori_loop(0, micro, forward, 0)

    pl.when(s >= last - lead)(exchange_early)

    scale = 1.0 / (ndp - 1.0)

    @pl.when(s >= last - lead)
    def _():
        for m in range(micro - 2):
            settle(m)

    settle(micro - 2)
    m = micro - 1
    for i in range(1, ndp // 2):
        q_wait(m, i)
    q_swap(m, plane).start()
    for i in range(1, ndp):
        y_wait(m, i)
    GO[...] = (GO[...] + dot_tn(DS[m], RA[m])) * scale
    out1 = pltpu.make_async_copy(GO, grad_out.at[0], loc.at[1])
    out1.start()
    q_swap(m, foreign).wait_recv()
    GI[...] = (GI[...] + dot_tn(XS[m], DQ[m])) * scale
    out2 = pltpu.make_async_copy(GI, grad_in.at[0], loc.at[2])
    out2.start()

    for copy in sent:
        copy.wait_send()
    for i in range(1, ndp):
        x_copy(i).wait_send()
    for i in range(1, ndp // 2):
        r_copy(i).wait_send()
    r_swap(plane).wait_send()

    def drain(m, carry):
        @pl.when(s > 0)
        def _():
            for k in range(nchunk):
                chunk_copy(m, k).wait_send()

        @pl.when(node)
        def _():
            for k in range(nchunk):
                pass_on(m, k).wait_send()

        for i in range(1, ndp // 2):
            q_copy(m, i).wait_send()
        q_swap(m, plane).wait_send()
        for i in range(1, ndp):
            y_copy(m, i).wait_send()
        return carry

    lax.fori_loop(0, micro, drain, 0)
    for copy in writes:
        copy.wait()
    out1.wait()
    out2.wait()


def shards(acts, out_grad, w_in, w_out, decay_rate, cycle_order):
    nsec = lax.axis_size("section")
    ndp = lax.axis_size("dp")
    _, micro, tok, width = acts.shape
    cols = w_out.shape[2]
    heads = decay_rate.shape[1]
    hd = cols // heads
    blk = width // ndp
    nchunk = 4
    dims = (nsec, ndp, micro, tok, width, heads, hd, nchunk)
    dma = pltpu.SemaphoreType.DMA
    any_spec = pl.BlockSpec(memory_space=pl.ANY)
    smem = pl.BlockSpec(memory_space=pltpu.SMEM)
    return pl.pallas_call(
        functools.partial(kernel, dims),
        name="retention_stack_back",
        out_shape=(
            jax.ShapeDtypeStruct((1, micro, tok, width), BF),
            jax.ShapeDtypeStruct((1, blk, 3 * cols), F32),
            jax.ShapeDtypeStruct((1, blk, cols), F32),
        ),
        in_specs=[any_spec] * 4 + [smem] * 2,
        out_specs=[any_spec] * 3,
        scratch_shapes=[
            pltpu.VMEM((ndp, blk, 3 * cols), BF),
            pltpu.VMEM((ndp, blk, cols), BF),
            pltpu.VMEM((ndp, 3 * cols, blk), BF),
            pltpu.VMEM((ndp, micro, tok, blk), BF),
            pltpu.VMEM((micro, ndp, tok, blk), BF),
            pltpu.VMEM((micro, ndp, tok, blk), BF),
            pltpu.VMEM((micro, ndp, tok, blk), BF),
            pltpu.VMEM((micro * tok, 3 * cols), F32),
            pltpu.VMEM((micro, tok, 3 * cols), BF),
            pltpu.VMEM((micro, heads, tok, tok), BF),
            pltpu.VMEM((heads, tok, tok), F32),
            pltpu.VMEM((micro, ndp * tok, blk), BF),
            pltpu.VMEM((micro, ndp * tok, blk), BF),
            pltpu.VMEM((micro, ndp * tok, 3 * cols), BF),
            pltpu.VMEM((micro, ndp * tok, cols), BF),
            pltpu.VMEM((blk, 3 * cols), F32),
            pltpu.VMEM((blk, cols), F32),
            dma((2 + ndp,)),
            dma((64,)),
            dma((ndp, 2, 2)),
            dma((micro, nchunk)),
            dma((micro, nchunk)),
            dma((micro, nchunk)),
            dma((micro, nchunk)),
            dma((ndp,)),
            dma((ndp,)),
            dma((ndp // 2,)),
            dma((ndp // 2,)),
            dma((micro, ndp // 2)),
            dma((micro, ndp // 2)),
            dma((micro, ndp)),
            dma((micro, ndp)),
            dma((ndp,)),
        ],
        compiler_params=pltpu.CompilerParams(
            collective_id=0, has_side_effects=True, vmem_limit_bytes=60 * 1024 * 1024
        ),
        cost_estimate=pl.CostEstimate(
            flops=6_000_000_000, bytes_accessed=8_000_000, transcendentals=4096
        ),
    )(acts, out_grad, w_in, w_out, decay_rate, cycle_order)


def solution(mesh):
    placed = (
        P("section", None, "dp", None),
        P(None, "dp", None),
        P("section", "dp", None),
        P("section", "dp", None),
        P("section", None),
        P(),
    )
    return jax.shard_map(
        shards,
        mesh=mesh,
        in_specs=placed,
        out_specs=(
            P("section", None, "dp", None),
            P("section", "dp", None),
            P("section", "dp", None),
        ),
        check_vma=False,
    )
```

```python
import functools

import jax
import jax.numpy as jnp
from jax import lax
from jax.experimental import pallas as pl
from jax.experimental.pallas import tpu as pltpu
from jax.sharding import PartitionSpec as P

MESH = pl.DeviceIdType.MESH
BF = jnp.bfloat16
F32 = jnp.float32


def dot(a, b):
    return jnp.dot(a, b, preferred_element_type=F32)


def dot_nt(a, b):
    return lax.dot_general(a, b, (((1,), (1,)), ((), ())), preferred_element_type=F32)


def dot_tn(a, b):
    return lax.dot_general(a, b, (((0,), (0,)), ((), ())), preferred_element_type=F32)


def kernel(
    dims,
    acts, out_grad, w_in, w_out, rates, order,
    in_grad, grad_in, grad_out,
    WI, WO, WT, XB, DY, NX, RB, ACC, QKV, SC, TAB, XS, DS, DQ, RA, GI, GO,
    loc, wsend, wrecv, csend, crecv, bsend, brecv, xsend, xrecv, rsend, rrecv, qsend, qrecv, ysend, yrecv, outsem,
):
    nsec, ndp, micro, tok, width, heads, hd, nchunk = dims
    cols = heads * hd
    blk = width // ndp
    half = blk // 2
    per = ndp // nchunk
    nx = ndp // 4
    s = lax.axis_index("section")
    r = lax.axis_index("dp")
    x, zl, c = r // 4, (r // 2) % 2, r % 2
    last = nsec - 1
    lead = min(4, nsec // 4)
    ny = 4 if nsec >= 16 else 2
    y = lax.rem(s, ny)
    to_relay = (s > 0) & (y == 0) & (zl == 0)
    to_next = (s > 0) & ((y != 0) | (zl != 0))
    node = (s >= ny) & (y == ny - 1) & (zl == 0)
    by_relay = (s < last) & (y == ny - 1) & (zl == 0)
    by_prev = (s < last) & ((y != ny - 1) | (zl != 0))
    slot = c * (ndp // 2) + r // 2

    def rep(xx, zz, cc):
        return lax.rem(xx + nx, nx) * 4 + zz * 2 + cc

    core, zp = rep(x, zl, 1 - c), rep(x, 1 - zl, c)
    xp, xm, xo = rep(x + 1, zl, c), rep(x - 1, zl, c), rep(x + 2, zl, c)
    xpz, xmz, xoz = rep(x + 1, 1 - zl, c), rep(x - 1, 1 - zl, c), rep(x + 2, 1 - zl, c)

    def peer(i):
        return lax.rem(r + i, ndp)

    def slot_of(q):
        return lax.rem(q, 2) * (ndp // 2) + q // 2

    local = [
        pltpu.make_async_copy(w_in.at[0], WI.at[r], loc.at[0]),
        pltpu.make_async_copy(w_out.at[0], WO.at[r], loc.at[1]),
    ]
    for i in range(ndp):
        local.append(
            pltpu.make_async_copy(
                acts.at[0, :, :, pl.ds(i * blk, blk)], XB.at[i], loc.at[2 + i]
            )
        )
    for copy in local:
        copy.start()

    barrier = pltpu.get_barrier_semaphore()
    for i in range(1, ndp):
        pl.semaphore_signal(barrier, inc=1, device_id=(s, peer(i)), device_id_type=MESH)

    def greet(cond, section):
        @pl.when(cond)
        def _():
            pl.semaphore_signal(
                barrier, inc=1, device_id=(section, r), device_id_type=MESH
            )

    greet(by_prev, jnp.minimum(s + 1, last))
    greet(by_relay, jnp.minimum(s + ny, last))
    greet(node, jnp.maximum(s - (ny - 1), 0))
    receivers = (
        jnp.where(to_next, 1, 0) + jnp.where(to_relay, 1, 0) + jnp.where(node, 1, 0)
    )
    pl.semaphore_wait(barrier, ndp - 1 + receivers)

    def piece(ref, q, h):
        return ref.at[q, pl.ds(h * half, half)]

    sent = []

    def push(q, h, target, own=False):
        for which, ref in enumerate((WI, WO)):
            if own:
                src = (w_in, w_out)[which].at[0, pl.ds(h * half, half)]
            else:
                src = piece(ref, q, h)
            copy = pltpu.make_async_remote_copy(
                src_ref=src,
                dst_ref=piece(ref, q, h),
                send_sem=wsend.at[len(sent)],
                recv_sem=wrecv.at[q, h, which],
                device_id=(s, target),
                device_id_type=MESH,
            )
            copy.start()
            sent.append(copy)

    def arrive(q, h):
        for which, ref in enumerate((WI, WO)):
            pltpu.make_async_remote_copy(
                src_ref=piece(ref, q, h),
                dst_ref=piece(ref, q, h),
                send_sem=wsend.at[0],
                recv_sem=wrecv.at[q, h, which],
                device_id=(s, core),
                device_id_type=MESH,
            ).wait_recv()

    for h in range(2):
        for target in (xp, xm, zp, core):
            push(r, h, target, own=True)

    ACC[...] = jnp.zeros_like(ACC)

    def add(q):
        ACC[...] += dot(XB[q].reshape(micro * tok, blk), WI[q])
        WT[q] = WI[q].T

    for copy in local:
        copy.wait()

    @pl.when(s == last)
    def _():
        for i in range(ndp):
            pltpu.make_async_copy(
                out_grad.at[:, :, pl.ds(i * blk, blk)], DY.at[:, i], outsem.at[i]
            ).start()

    spot_t = lax.broadcasted_iota(jnp.int32, (tok, tok), 0)
    spot_j = lax.broadcasted_iota(jnp.int32, (tok, tok), 1)
    offset = (spot_t - spot_j).astype(F32)
    for h in range(heads):
        decayed = jnp.exp(-rates[0, h] * jnp.maximum(offset, 0.0))
        TAB[h] = jnp.where(offset >= 0.0, decayed, 0.0)

    add(r)
    arrive(xm, 0)
    push(xm, 0, xp)
    push(xm, 0, core)
    arrive(xp, 0)
    push(xp, 0, core)
    arrive(zp, 0)
    push(zp, 0, xp)
    push(zp, 0, xm)
    push(zp, 0, core)
    arrive(core, 0)
    arrive(core, 1)
    add(core)
    arrive(xp, 1)
    push(xp, 1, xm)
    push(xp, 1, core)
    arrive(xm, 1)
    push(xm, 1, core)
    arrive(zp, 1)
    push(zp, 1, xp)
    push(zp, 1, xm)
    push(zp, 1, core)
    add(xm)
    add(xp)
    add(zp)
    arrive(xo, 0)
    push(xo, 0, zp)
    push(xo, 0, core)
    arrive(xo, 1)
    push(xo, 1, zp)
    push(xo, 1, core)

    def other(q):
        return q + 1 - 2 * c

    for q in (xm, xp, zp):
        arrive(other(q), 0)
        arrive(other(q), 1)
        add(other(q))
    add(xo)
    for q in (xmz, xpz):
        for h in range(2):
            arrive(q, h)
            push(q, h, core)
    arrive(xoz, 0)
    push(xoz, 0, core)
    add(xmz)
    add(xpz)
    arrive(xoz, 1)
    push(xoz, 1, core)
    for q in (xo, xmz, xpz):
        arrive(other(q), 0)
        arrive(other(q), 1)
        add(other(q))
    add(xoz)
    arrive(other(xoz), 0)
    arrive(other(xoz), 1)
    add(other(xoz))

    failed = order[ndp - 1]
    live = jnp.where(r == failed, 0.0, 1.0).astype(F32)
    mine = pl.ds(pl.multiple_of(slot * tok, tok), tok)

    QKV[...] = ACC[...].astype(BF).reshape(micro, tok, 3 * cols)
    for m in range(micro):
        for h in range(heads):
            q = QKV[m, :, h * hd : (h + 1) * hd]
            k = QKV[m, :, cols + h * hd : cols + (h + 1) * hd]
            v = QKV[m, :, 2 * cols + h * hd : 2 * cols + (h + 1) * hd]
            score = (dot_nt(q, k) * TAB[h] / hd).astype(BF)
            SC[m, h] = score
            mixed = dot(score, v).astype(BF)
            RA[m, mine, h * hd : (h + 1) * hd] = (mixed.astype(F32) * live).astype(BF)

    plane = pl.ds(pl.multiple_of(c * (ndp // 2) * tok, tok), (ndp // 2) * tok)
    foreign = pl.ds(pl.multiple_of((1 - c) * (ndp // 2) * tok, tok), (ndp // 2) * tok)

    def rows_of(q):
        return pl.ds(pl.multiple_of(slot_of(q) * tok, tok), tok)

    def x_copy(i):
        q = peer(i)
        return pltpu.make_async_remote_copy(
            src_ref=XB.at[q], dst_ref=XS.at[:, mine],
            send_sem=xsend.at[i], recv_sem=xrecv.at[i],
            device_id=(s, q), device_id_type=MESH,
        )

    def x_wait(i):
        q = lax.rem(r - i + ndp, ndp)
        pltpu.make_async_remote_copy(
            src_ref=XB.at[q], dst_ref=XS.at[:, rows_of(q)],
            send_sem=xsend.at[i], recv_sem=xrecv.at[i],
            device_id=(s, q), device_id_type=MESH,
        ).wait_recv()

    def r_copy(i):
        q = peer(2 * i)
        return pltpu.make_async_remote_copy(
            src_ref=RA.at[:, mine], dst_ref=RA.at[:, mine],
            send_sem=rsend.at[i], recv_sem=rrecv.at[i],
            device_id=(s, q), device_id_type=MESH,
        )

    def r_wait(i):
        q = lax.rem(r - 2 * i + ndp, ndp)
        pltpu.make_async_remote_copy(
            src_ref=RA.at[:, rows_of(q)], dst_ref=RA.at[:, rows_of(q)],
            send_sem=rsend.at[i], recv_sem=rrecv.at[i],
            device_id=(s, q), device_id_type=MESH,
        ).wait_recv()

    def r_swap(rows):
        return pltpu.make_async_remote_copy(
            src_ref=RA.at[:, rows], dst_ref=RA.at[:, rows],
            send_sem=rsend.at[0], recv_sem=rrecv.at[0],
            device_id=(s, core), device_id_type=MESH,
        )

    own_x = pltpu.make_async_copy(XB.at[r], XS.at[:, mine], loc.at[0])

    def exchange_early():
        for i in range(1, ndp // 2):
            r_copy(i).start()
        own_x.start()
        for i in range(1, ndp):
            x_copy(i).start()
        for i in range(1, ndp // 2):
            r_wait(i)
        r_swap(plane).start()
        own_x.wait()
        for i in range(1, ndp):
            x_wait(i)
        r_swap(foreign).wait_recv()

    GI[...] = jnp.zeros_like(GI)
    GO[...] = jnp.zeros_like(GO)
    early = s < last - lead
    pl.when(early)(exchange_early)

    def chunk_copy(m, k):
        part = pl.ds(k * per, per)
        return pltpu.make_async_remote_copy(
            src_ref=NX.at[m, part], dst_ref=DY.at[m, part],
            send_sem=csend.at[m, k], recv_sem=crecv.at[m, k],
            device_id=(jnp.maximum(s - 1, 0), r), device_id_type=MESH,
        )

    def relay_copy(m, k):
        part = pl.ds(k * per, per)
        return pltpu.make_async_remote_copy(
            src_ref=NX.at[m, part], dst_ref=RB.at[m, part],
            send_sem=csend.at[m, k], recv_sem=brecv.at[m, k],
            device_id=(jnp.minimum(s + ny - 1, last), r), device_id_type=MESH,
        )

    def pass_on(m, k):
        part = pl.ds(k * per, per)
        return pltpu.make_async_remote_copy(
            src_ref=RB.at[m, part], dst_ref=DY.at[m, part],
            send_sem=bsend.at[m, k], recv_sem=crecv.at[m, k],
            device_id=(jnp.maximum(s - ny, 0), r), device_id_type=MESH,
        )

    def q_copy(m, i):
        q = peer(2 * i)
        return pltpu.make_async_remote_copy(
            src_ref=DQ.at[m, mine], dst_ref=DQ.at[m, mine],
            send_sem=qsend.at[m, i], recv_sem=qrecv.at[m, i],
            device_id=(s, q), device_id_type=MESH,
        )

    def q_wait(m, i):
        q = lax.rem(r - 2 * i + ndp, ndp)
        pltpu.make_async_remote_copy(
            src_ref=DQ.at[m, rows_of(q)], dst_ref=DQ.at[m, rows_of(q)],
            send_sem=qsend.at[m, i], recv_sem=qrecv.at[m, i],
            device_id=(s, q), device_id_type=MESH,
        ).wait_recv()

    def q_swap(m, rows):
        return pltpu.make_async_remote_copy(
            src_ref=DQ.at[m, rows], dst_ref=DQ.at[m, rows],
            send_sem=qsend.at[m, 0], recv_sem=qrecv.at[m, 0],
            device_id=(s, core), device_id_type=MESH,
        )

    def y_copy(m, i):
        q = peer(i)
        return pltpu.make_async_remote_copy(
            src_ref=DY.at[m, q], dst_ref=DS.at[m, mine],
            send_sem=ysend.at[m, i], recv_sem=yrecv.at[m, i],
            device_id=(s, q), device_id_type=MESH,
        )

    def y_wait(m, i):
        q = lax.rem(r - i + ndp, ndp)
        pltpu.make_async_remote_copy(
            src_ref=DY.at[m, q], dst_ref=DS.at[m, rows_of(q)],
            send_sem=ysend.at[m, i], recv_sem=yrecv.at[m, i],
            device_id=(s, q), device_id_type=MESH,
        ).wait_recv()

    @pl.when(s == last)
    def _():
        for i in range(ndp):
            pltpu.make_async_copy(
                out_grad.at[:, :, pl.ds(i * blk, blk)], DY.at[:, i], outsem.at[i]
            ).wait()

    def settle(m):
        q_swap(m, foreign).wait_recv()
        for i in range(1, ndp):
            y_wait(m, i)
        GI[...] += dot_tn(XS[m], DQ[m])
        GO[...] += dot_tn(DS[m], RA[m])

    def exchange(m):
        for i in range(1, ndp // 2):
            q_copy(m, i).start()
        for i in range(1, ndp):
            y_copy(m, i).start()

    inline = s < nsec // 3 + 1

    def step(m, carry):
        d_mixed = jnp.zeros((tok, cols), F32)
        for k in range(nchunk):
            @pl.when(s < last)
            def _():
                chunk_copy(m, k).wait_recv()

            for j in range(k * per, (k + 1) * per):
                d_mixed += dot(DY[m, j], WO[j])
        d_mixed = d_mixed.astype(BF)
        parts = [[], [], []]
        for h in range(heads):
            q = QKV[m, :, h * hd : (h + 1) * hd]
            k = QKV[m, :, cols + h * hd : cols + (h + 1) * hd]
            v = QKV[m, :, 2 * cols + h * hd : 2 * cols + (h + 1) * hd]
            dr = d_mixed[:, h * hd : (h + 1) * hd]
            d_score = (dot_nt(dr, v) * TAB[h] / hd).astype(BF)
            parts[0].append(dot(d_score, k).astype(BF))
            parts[1].append(dot_tn(d_score, q).astype(BF))
            parts[2].append(dot_tn(SC[m, h], dr).astype(BF))
        d_all = jnp.concatenate(parts[0] + parts[1] + parts[2], axis=1)
        for k in range(nchunk):
            for j in range(k * per, (k + 1) * per):
                back = dot(d_all, WT[j])
                NX[m, j] = (DY[m, j].astype(F32) + back).astype(BF)

            @pl.when(to_next)
            def _():
                chunk_copy(m, k).start()

            @pl.when(to_relay)
            def _():
                relay_copy(m, k).start()

        DQ[m, mine] = (d_all.astype(F32) * live).astype(BF)
        DS[m, mine] = DY[m, r]

        @pl.when(inline)
        def _():
            exchange(m)

        return carry

    lax.fori_loop(0, micro, step, 0)
    writes = [
        pltpu.make_async_copy(
            NX.at[:, i], in_grad.at[0, :, :, pl.ds(i * blk, blk)], outsem.at[i]
        )
        for i in range(ndp)
    ]
    for copy in writes:
        copy.start()

    @pl.when(node)
    def _():
        def forward(m, carry):
            for k in range(nchunk):
                relay_copy(m, k).wait_recv()
                pass_on(m, k).start()
            return carry

        lax.fori_loop(0, micro, forward, 0)

    pl.when(s >= last - lead)(exchange_early)

    @pl.when(s >= nsec // 3 + 1)
    def _():
        def send(m, carry):
            exchange(m)
            return carry

        lax.fori_loop(0, micro, send, 0)

    scale = 1.0 / (ndp - 1.0)

    def swap(m):
        for i in range(1, ndp // 2):
            q_wait(m, i)
        q_swap(m, plane).start()

    swap(0)

    def finish(m, carry):
        swap(m + 1)
        settle(m)
        return carry

    lax.fori_loop(0, micro - 1, finish, 0)
    m = micro - 1
    for i in range(1, ndp):
        y_wait(m, i)
    GO[...] = (GO[...] + dot_tn(DS[m], RA[m])) * scale
    out1 = pltpu.make_async_copy(GO, grad_out.at[0], loc.at[1])
    out1.start()
    q_swap(m, foreign).wait_recv()
    GI[...] = (GI[...] + dot_tn(XS[m], DQ[m])) * scale
    out2 = pltpu.make_async_copy(GI, grad_in.at[0], loc.at[2])
    out2.start()

    for copy in sent:
        copy.wait_send()
    for i in range(1, ndp):
        x_copy(i).wait_send()
    for i in range(1, ndp // 2):
        r_copy(i).wait_send()
    r_swap(plane).wait_send()

    def drain(m, carry):
        @pl.when(s > 0)
        def _():
            for k in range(nchunk):
                chunk_copy(m, k).wait_send()

        @pl.when(node)
        def _():
            for k in range(nchunk):
                pass_on(m, k).wait_send()

        for i in range(1, ndp // 2):
            q_copy(m, i).wait_send()
        q_swap(m, plane).wait_send()
        for i in range(1, ndp):
            y_copy(m, i).wait_send()
        return carry

    lax.fori_loop(0, micro, drain, 0)
    for copy in writes:
        copy.wait()
    out1.wait()
    out2.wait()


def shards(acts, out_grad, w_in, w_out, decay_rate, cycle_order):
    nsec = lax.axis_size("section")
    ndp = lax.axis_size("dp")
    _, micro, tok, width = acts.shape
    cols = w_out.shape[2]
    heads = decay_rate.shape[1]
    hd = cols // heads
    blk = width // ndp
    nchunk = 4
    dims = (nsec, ndp, micro, tok, width, heads, hd, nchunk)
    dma = pltpu.SemaphoreType.DMA
    any_spec = pl.BlockSpec(memory_space=pl.ANY)
    smem = pl.BlockSpec(memory_space=pltpu.SMEM)
    return pl.pallas_call(
        functools.partial(kernel, dims),
        name="retention_stack_back",
        out_shape=(
            jax.ShapeDtypeStruct((1, micro, tok, width), BF),
            jax.ShapeDtypeStruct((1, blk, 3 * cols), F32),
            jax.ShapeDtypeStruct((1, blk, cols), F32),
        ),
        in_specs=[any_spec] * 4 + [smem] * 2,
        out_specs=[any_spec] * 3,
        scratch_shapes=[
            pltpu.VMEM((ndp, blk, 3 * cols), BF),
            pltpu.VMEM((ndp, blk, cols), BF),
            pltpu.VMEM((ndp, 3 * cols, blk), BF),
            pltpu.VMEM((ndp, micro, tok, blk), BF),
            pltpu.VMEM((micro, ndp, tok, blk), BF),
            pltpu.VMEM((micro, ndp, tok, blk), BF),
            pltpu.VMEM((micro, ndp, tok, blk), BF),
            pltpu.VMEM((micro * tok, 3 * cols), F32),
            pltpu.VMEM((micro, tok, 3 * cols), BF),
            pltpu.VMEM((micro, heads, tok, tok), BF),
            pltpu.VMEM((heads, tok, tok), F32),
            pltpu.VMEM((micro, ndp * tok, blk), BF),
            pltpu.VMEM((micro, ndp * tok, blk), BF),
            pltpu.VMEM((micro, ndp * tok, 3 * cols), BF),
            pltpu.VMEM((micro, ndp * tok, cols), BF),
            pltpu.VMEM((blk, 3 * cols), F32),
            pltpu.VMEM((blk, cols), F32),
            dma((2 + ndp,)),
            dma((64,)),
            dma((ndp, 2, 2)),
            dma((micro, nchunk)),
            dma((micro, nchunk)),
            dma((micro, nchunk)),
            dma((micro, nchunk)),
            dma((ndp,)),
            dma((ndp,)),
            dma((ndp // 2,)),
            dma((ndp // 2,)),
            dma((micro, ndp // 2)),
            dma((micro, ndp // 2)),
            dma((micro, ndp)),
            dma((micro, ndp)),
            dma((ndp,)),
        ],
        compiler_params=pltpu.CompilerParams(
            collective_id=0, has_side_effects=True, vmem_limit_bytes=60 * 1024 * 1024
        ),
        cost_estimate=pl.CostEstimate(
            flops=6_000_000_000, bytes_accessed=8_000_000, transcendentals=4096
        ),
    )(acts, out_grad, w_in, w_out, decay_rate, cycle_order)


def solution(mesh):
    placed = (
        P("section", None, "dp", None),
        P(None, "dp", None),
        P("section", "dp", None),
        P("section", "dp", None),
        P("section", None),
        P(),
    )
    return jax.shard_map(
        shards,
        mesh=mesh,
        in_specs=placed,
        out_specs=(
            P("section", None, "dp", None),
            P("section", "dp", None),
            P("section", "dp", None),
        ),
        check_vma=False,
    )
```

```python
import functools

import jax
import jax.numpy as jnp
from jax import lax
from jax.experimental import pallas as pl
from jax.experimental.pallas import tpu as pltpu
from jax.sharding import PartitionSpec as P

MESH = pl.DeviceIdType.MESH
BF = jnp.bfloat16
F32 = jnp.float32


def dot(a, b):
    return jnp.dot(a, b, preferred_element_type=F32)


def dot_nt(a, b):
    return lax.dot_general(a, b, (((1,), (1,)), ((), ())), preferred_element_type=F32)


def dot_tn(a, b):
    return lax.dot_general(a, b, (((0,), (0,)), ((), ())), preferred_element_type=F32)


def kernel(
    dims,
    acts, out_grad, w_in, w_out, rates, order,
    in_grad, grad_in, grad_out,
    WI, WS, WO, WT, MA, MM, DRB, DRN, RD, PA, XB, DY, NX, RB, ACC, QKV, SC, TAB, XS, DS, DQ, RA, GI, GO,
    loc, wsend, wrecv, csend, crecv, bsend, brecv, dsend, drecv, esend, erecv, xsend, xrecv, rsend, rrecv, qsend, qrecv, ysend, yrecv, outsem,
):
    nsec, ndp, micro, tok, width, heads, hd, nchunk = dims
    cols = heads * hd
    blk = width // ndp
    half = blk // 2
    per = ndp // nchunk
    nx = ndp // 4
    s = lax.axis_index("section")
    r = lax.axis_index("dp")
    x, zl, c = r // 4, (r // 2) % 2, r % 2
    last = nsec - 1
    lead = min(4, nsec // 4)
    ny = 4 if nsec >= 16 else 2
    y = lax.rem(s, ny)
    direct = s >= last - 1
    ahead = (s > 0) & (s < last)
    to_relay = (s > 0) & (y == 0) & (zl == 0)
    to_next = (s > 0) & ((y != 0) | (zl != 0))
    node = (s >= ny) & (y == ny - 1) & (zl == 0)
    by_relay = (s < last) & (y == ny - 1) & (zl == 0)
    by_prev = (s < last) & ((y != ny - 1) | (zl != 0))
    slot = c * (ndp // 2) + r // 2

    def rep(xx, zz, cc):
        return lax.rem(xx + nx, nx) * 4 + zz * 2 + cc

    core, zp = rep(x, zl, 1 - c), rep(x, 1 - zl, c)
    xp, xm, xo = rep(x + 1, zl, c), rep(x - 1, zl, c), rep(x + 2, zl, c)
    xpz, xmz, xoz = rep(x + 1, 1 - zl, c), rep(x - 1, 1 - zl, c), rep(x + 2, 1 - zl, c)

    def peer(i):
        return lax.rem(r + i, ndp)

    def slot_of(q):
        return lax.rem(q, 2) * (ndp // 2) + q // 2

    local = [
        pltpu.make_async_copy(w_in.at[0], WI.at[r], loc.at[0]),
        pltpu.make_async_copy(w_out.at[0], WS.at[r], loc.at[1]),
    ]
    for i in range(ndp):
        local.append(
            pltpu.make_async_copy(
                acts.at[0, :, :, pl.ds(i * blk, blk)], XB.at[i], loc.at[2 + i]
            )
        )
    for copy in local:
        copy.start()

    barrier = pltpu.get_barrier_semaphore()
    for i in range(1, ndp):
        pl.semaphore_signal(barrier, inc=1, device_id=(s, peer(i)), device_id_type=MESH)

    def greet(cond, section):
        @pl.when(cond)
        def _():
            pl.semaphore_signal(
                barrier, inc=1, device_id=(section, r), device_id_type=MESH
            )

    greet(by_prev, jnp.minimum(s + 1, last))
    greet(by_relay, jnp.minimum(s + ny, last))
    greet(node, jnp.maximum(s - (ny - 1), 0))
    greet(ahead, jnp.maximum(s - 1, 0))
    receivers = (
        jnp.where(to_next, 1, 0)
        + jnp.where(to_relay, 1, 0)
        + jnp.where(node, 1, 0)
        + jnp.where(s < last - 1, 1, 0)
    )
    pl.semaphore_wait(barrier, ndp - 1 + receivers)

    def piece(ref, q, h):
        return ref.at[q, pl.ds(h * half, half)]

    sent = []
    needed = (s >= 0, direct, ahead)

    def push(q, h, target, arrays=(0, 1, 2), own=False):
        for which in arrays:
            ref = (WI, WS, WO)[which]
            src = piece(ref, q, h)
            if own and which < 2:
                src = (w_in, w_out)[which].at[0, pl.ds(h * half, half)]
            copy = pltpu.make_async_remote_copy(
                src_ref=src,
                dst_ref=piece(ref, q, h),
                send_sem=wsend.at[len(sent)],
                recv_sem=wrecv.at[q, h, which],
                device_id=(s, target),
                device_id_type=MESH,
            )
            sent.append((copy, needed[which]))
            pl.when(needed[which])(copy.start)

    def arrive(q, h):
        for which, ref in enumerate((WI, WS, WO)):
            copy = pltpu.make_async_remote_copy(
                src_ref=piece(ref, q, h),
                dst_ref=piece(ref, q, h),
                send_sem=wsend.at[0],
                recv_sem=wrecv.at[q, h, which],
                device_id=(s, core),
                device_id_type=MESH,
            )
            pl.when(needed[which])(copy.wait_recv)

    def up_copy(h):
        return pltpu.make_async_remote_copy(
            src_ref=w_out.at[0, pl.ds(h * half, half)],
            dst_ref=piece(WO, r, h),
            send_sem=loc.at[2 + ndp + h],
            recv_sem=wrecv.at[r, h, 2],
            device_id=(jnp.minimum(s + 1, last), r),
            device_id_type=MESH,
        )

    for h in range(2):
        pl.when(s < last - 1)(up_copy(h).start)
    for h in range(2):
        for target in (xp, xm, zp, core):
            push(r, h, target, arrays=(0, 1), own=True)

    MA[...] = jnp.zeros_like(MA)
    ACC[...] = jnp.zeros_like(ACC)

    def fold(q):
        MA[...] += dot(WT[q], WO[q])

    def add(q):
        ACC[...] += dot(XB[q].reshape(micro * tok, blk), WI[q])
        WT[q] = WI[q].T
        pl.when(ahead)(functools.partial(fold, q))

    for copy in local:
        copy.wait()

    @pl.when(s == last)
    def _():
        for i in range(ndp):
            pltpu.make_async_copy(
                out_grad.at[:, :, pl.ds(i * blk, blk)], DY.at[:, i], outsem.at[i]
            ).start()

    spot_t = lax.broadcasted_iota(jnp.int32, (tok, tok), 0)
    spot_j = lax.broadcasted_iota(jnp.int32, (tok, tok), 1)
    offset = (spot_t - spot_j).astype(F32)
    for h in range(heads):
        decayed = jnp.exp(-rates[0, h] * jnp.maximum(offset, 0.0))
        TAB[h] = jnp.where(offset >= 0.0, decayed, 0.0)

    @pl.when(ahead)
    def _():
        for h in range(2):
            up_copy(h).wait_recv()

    for h in range(2):
        for target in (xp, xm, zp, core):
            push(r, h, target, arrays=(2,))
    add(r)
    arrive(xm, 0)
    push(xm, 0, xp)
    push(xm, 0, core)
    arrive(xp, 0)
    push(xp, 0, core)
    arrive(zp, 0)
    push(zp, 0, xp)
    push(zp, 0, xm)
    push(zp, 0, core)
    arrive(core, 0)
    arrive(core, 1)
    add(core)
    arrive(xp, 1)
    push(xp, 1, xm)
    push(xp, 1, core)
    arrive(xm, 1)
    push(xm, 1, core)
    arrive(zp, 1)
    push(zp, 1, xp)
    push(zp, 1, xm)
    push(zp, 1, core)
    add(xm)
    add(xp)
    add(zp)
    arrive(xo, 0)
    push(xo, 0, zp)
    push(xo, 0, core)
    arrive(xo, 1)
    push(xo, 1, zp)
    push(xo, 1, core)

    def other(q):
        return q + 1 - 2 * c

    for q in (xm, xp, zp):
        arrive(other(q), 0)
        arrive(other(q), 1)
        add(other(q))
    add(xo)
    for q in (xmz, xpz):
        for h in range(2):
            arrive(q, h)
            push(q, h, core)
    arrive(xoz, 0)
    push(xoz, 0, core)
    add(xmz)
    add(xpz)
    arrive(xoz, 1)
    push(xoz, 1, core)
    for q in (xo, xmz, xpz):
        arrive(other(q), 0)
        arrive(other(q), 1)
        add(other(q))
    add(xoz)
    arrive(other(xoz), 0)
    arrive(other(xoz), 1)
    add(other(xoz))

    MM[...] = MA[...].astype(BF)
    failed = order[ndp - 1]
    live = jnp.where(r == failed, 0.0, 1.0).astype(F32)
    mine = pl.ds(pl.multiple_of(slot * tok, tok), tok)

    QKV[...] = ACC[...].astype(BF).reshape(micro, tok, 3 * cols)
    for m in range(micro):
        for h in range(heads):
            q = QKV[m, :, h * hd : (h + 1) * hd]
            k = QKV[m, :, cols + h * hd : cols + (h + 1) * hd]
            v = QKV[m, :, 2 * cols + h * hd : 2 * cols + (h + 1) * hd]
            score = (dot_nt(q, k) * TAB[h] / hd).astype(BF)
            SC[m, h] = score
            mixed = dot(score, v).astype(BF)
            RA[m, mine, h * hd : (h + 1) * hd] = (mixed.astype(F32) * live).astype(BF)

    plane = pl.ds(pl.multiple_of(c * (ndp // 2) * tok, tok), (ndp // 2) * tok)
    foreign = pl.ds(pl.multiple_of((1 - c) * (ndp // 2) * tok, tok), (ndp // 2) * tok)

    def rows_of(q):
        return pl.ds(pl.multiple_of(slot_of(q) * tok, tok), tok)

    def x_copy(i):
        q = peer(i)
        return pltpu.make_async_remote_copy(
            src_ref=XB.at[q], dst_ref=XS.at[:, mine],
            send_sem=xsend.at[i], recv_sem=xrecv.at[i],
            device_id=(s, q), device_id_type=MESH,
        )

    def x_wait(i):
        q = lax.rem(r - i + ndp, ndp)
        pltpu.make_async_remote_copy(
            src_ref=XB.at[q], dst_ref=XS.at[:, rows_of(q)],
            send_sem=xsend.at[i], recv_sem=xrecv.at[i],
            device_id=(s, q), device_id_type=MESH,
        ).wait_recv()

    def r_copy(i):
        q = peer(2 * i)
        return pltpu.make_async_remote_copy(
            src_ref=RA.at[:, mine], dst_ref=RA.at[:, mine],
            send_sem=rsend.at[i], recv_sem=rrecv.at[i],
            device_id=(s, q), device_id_type=MESH,
        )

    def r_wait(i):
        q = lax.rem(r - 2 * i + ndp, ndp)
        pltpu.make_async_remote_copy(
            src_ref=RA.at[:, rows_of(q)], dst_ref=RA.at[:, rows_of(q)],
            send_sem=rsend.at[i], recv_sem=rrecv.at[i],
            device_id=(s, q), device_id_type=MESH,
        ).wait_recv()

    def r_swap(rows):
        return pltpu.make_async_remote_copy(
            src_ref=RA.at[:, rows], dst_ref=RA.at[:, rows],
            send_sem=rsend.at[0], recv_sem=rrecv.at[0],
            device_id=(s, core), device_id_type=MESH,
        )

    own_x = pltpu.make_async_copy(XB.at[r], XS.at[:, mine], loc.at[0])

    def exchange_early():
        for i in range(1, ndp // 2):
            r_copy(i).start()
        own_x.start()
        for i in range(1, ndp):
            x_copy(i).start()
        for i in range(1, ndp // 2):
            r_wait(i)
        r_swap(plane).start()
        own_x.wait()
        for i in range(1, ndp):
            x_wait(i)
        r_swap(foreign).wait_recv()

    GI[...] = jnp.zeros_like(GI)
    GO[...] = jnp.zeros_like(GO)
    early = s < last - lead
    pl.when(early)(exchange_early)

    def chunk_copy(m, k):
        part = pl.ds(k * per, per)
        return pltpu.make_async_remote_copy(
            src_ref=NX.at[m, part], dst_ref=DY.at[m, part],
            send_sem=csend.at[m, k], recv_sem=crecv.at[m, k],
            device_id=(jnp.maximum(s - 1, 0), r), device_id_type=MESH,
        )

    def relay_copy(m, k):
        part = pl.ds(k * per, per)
        return pltpu.make_async_remote_copy(
            src_ref=NX.at[m, part], dst_ref=RB.at[m, part],
            send_sem=csend.at[m, k], recv_sem=brecv.at[m, k],
            device_id=(jnp.minimum(s + ny - 1, last), r), device_id_type=MESH,
        )

    def pass_on(m, k):
        part = pl.ds(k * per, per)
        return pltpu.make_async_remote_copy(
            src_ref=RB.at[m, part], dst_ref=DY.at[m, part],
            send_sem=bsend.at[m, k], recv_sem=crecv.at[m, k],
            device_id=(jnp.maximum(s - ny, 0), r), device_id_type=MESH,
        )

    def dr_copy(m):
        return pltpu.make_async_remote_copy(
            src_ref=DRN.at[m], dst_ref=DRB.at[m],
            send_sem=dsend.at[m], recv_sem=drecv.at[m],
            device_id=(jnp.maximum(s - 1, 0), r), device_id_type=MESH,
        )

    def dr_relay(m):
        return pltpu.make_async_remote_copy(
            src_ref=DRN.at[m], dst_ref=RD.at[m],
            send_sem=dsend.at[m], recv_sem=erecv.at[m],
            device_id=(jnp.minimum(s + ny - 1, last), r), device_id_type=MESH,
        )

    def dr_pass(m):
        return pltpu.make_async_remote_copy(
            src_ref=RD.at[m], dst_ref=DRB.at[m],
            send_sem=esend.at[m], recv_sem=drecv.at[m],
            device_id=(jnp.maximum(s - ny, 0), r), device_id_type=MESH,
        )

    def q_copy(m, i):
        q = peer(2 * i)
        return pltpu.make_async_remote_copy(
            src_ref=DQ.at[m, mine], dst_ref=DQ.at[m, mine],
            send_sem=qsend.at[m, i], recv_sem=qrecv.at[m, i],
            device_id=(s, q), device_id_type=MESH,
        )

    def q_wait(m, i):
        q = lax.rem(r - 2 * i + ndp, ndp)
        pltpu.make_async_remote_copy(
            src_ref=DQ.at[m, rows_of(q)], dst_ref=DQ.at[m, rows_of(q)],
            send_sem=qsend.at[m, i], recv_sem=qrecv.at[m, i],
            device_id=(s, q), device_id_type=MESH,
        ).wait_recv()

    def q_swap(m, rows):
        return pltpu.make_async_remote_copy(
            src_ref=DQ.at[m, rows], dst_ref=DQ.at[m, rows],
            send_sem=qsend.at[m, 0], recv_sem=qrecv.at[m, 0],
            device_id=(s, core), device_id_type=MESH,
        )

    def y_copy(m, i):
        q = peer(i)
        return pltpu.make_async_remote_copy(
            src_ref=DY.at[m, q], dst_ref=DS.at[m, mine],
            send_sem=ysend.at[m, i], recv_sem=yrecv.at[m, i],
            device_id=(s, q), device_id_type=MESH,
        )

    def y_wait(m, i):
        q = lax.rem(r - i + ndp, ndp)
        pltpu.make_async_remote_copy(
            src_ref=DY.at[m, q], dst_ref=DS.at[m, rows_of(q)],
            send_sem=ysend.at[m, i], recv_sem=yrecv.at[m, i],
            device_id=(s, q), device_id_type=MESH,
        ).wait_recv()

    @pl.when(s == last)
    def _():
        for i in range(ndp):
            pltpu.make_async_copy(
                out_grad.at[:, :, pl.ds(i * blk, blk)], DY.at[:, i], outsem.at[i]
            ).wait()

    def settle(m):
        q_swap(m, foreign).wait_recv()
        for i in range(1, ndp):
            y_wait(m, i)
        GI[...] += dot_tn(XS[m], DQ[m])
        GO[...] += dot_tn(DS[m], RA[m])

    def exchange(m):
        for i in range(1, ndp // 2):
            q_copy(m, i).start()
        for i in range(1, ndp):
            y_copy(m, i).start()

    inline = s < nsec // 3 + 1

    def step(m, carry):
        @pl.when(direct)
        def _():
            total = jnp.zeros((tok, cols), F32)
            for k in range(nchunk):
                pl.when(s < last)(chunk_copy(m, k).wait_recv)
                for j in range(k * per, (k + 1) * per):
                    total += dot(DY[m, j], WS[j])
            DRB[m] = total.astype(BF)

        pl.when(s < last - 1)(dr_copy(m).wait_recv)
        d_mixed = DRB[m]
        parts = [[], [], []]
        for h in range(heads):
            q = QKV[m, :, h * hd : (h + 1) * hd]
            k = QKV[m, :, cols + h * hd : cols + (h + 1) * hd]
            v = QKV[m, :, 2 * cols + h * hd : 2 * cols + (h + 1) * hd]
            dr = d_mixed[:, h * hd : (h + 1) * hd]
            d_score = (dot_nt(dr, v) * TAB[h] / hd).astype(BF)
            parts[0].append(dot(d_score, k).astype(BF))
            parts[1].append(dot_tn(d_score, q).astype(BF))
            parts[2].append(dot_tn(SC[m, h], dr).astype(BF))
        d_all = jnp.concatenate(parts[0] + parts[1] + parts[2], axis=1)

        @pl.when(ahead)
        def _():
            PA[...] = dot(d_all, MM[...])

        for k in range(nchunk):
            pl.when(s < last - 1)(chunk_copy(m, k).wait_recv)

            @pl.when(ahead)
            def _():
                total = PA[...]
                for j in range(k * per, (k + 1) * per):
                    total += dot(DY[m, j], WO[j])
                if k < nchunk - 1:
                    PA[...] = total
                else:
                    DRN[m] = total.astype(BF)
                    pl.when(to_next)(dr_copy(m).start)
                    pl.when(to_relay)(dr_relay(m).start)

            for j in range(k * per, (k + 1) * per):
                back = dot(d_all, WT[j])
                NX[m, j] = (DY[m, j].astype(F32) + back).astype(BF)

            @pl.when(to_next)
            def _():
                chunk_copy(m, k).start()

            @pl.when(to_relay)
            def _():
                relay_copy(m, k).start()

        DQ[m, mine] = (d_all.astype(F32) * live).astype(BF)
        DS[m, mine] = DY[m, r]

        @pl.when(inline)
        def _():
            exchange(m)

        return carry

    lax.fori_loop(0, micro, step, 0)
    writes = [
        pltpu.make_async_copy(
            NX.at[:, i], in_grad.at[0, :, :, pl.ds(i * blk, blk)], outsem.at[i]
        )
        for i in range(ndp)
    ]
    for copy in writes:
        copy.start()

    @pl.when(node)
    def _():
        def forward(m, carry):
            for k in range(nchunk):
                if k == nchunk - 1:
                    dr_relay(m).wait_recv()
                    dr_pass(m).start()
                relay_copy(m, k).wait_recv()
                pass_on(m, k).start()
            return carry

        lax.fori_loop(0, micro, forward, 0)

    pl.when(s >= last - lead)(exchange_early)

    @pl.when(s >= nsec // 3 + 1)
    def _():
        def send(m, carry):
            exchange(m)
            return carry

        lax.fori_loop(0, micro, send, 0)

    scale = 1.0 / (ndp - 1.0)

    def swap(m):
        for i in range(1, ndp // 2):
            q_wait(m, i)
        q_swap(m, plane).start()

    swap(0)

    def finish(m, carry):
        swap(m + 1)
        settle(m)
        return carry

    lax.fori_loop(0, micro - 1, finish, 0)
    m = micro - 1
    for i in range(1, ndp):
        y_wait(m, i)
    GO[...] = (GO[...] + dot_tn(DS[m], RA[m])) * scale
    out1 = pltpu.make_async_copy(GO, grad_out.at[0], loc.at[1])
    out1.start()
    q_swap(m, foreign).wait_recv()
    GI[...] = (GI[...] + dot_tn(XS[m], DQ[m])) * scale
    out2 = pltpu.make_async_copy(GI, grad_in.at[0], loc.at[2])
    out2.start()

    for copy, cond in sent:
        pl.when(cond)(copy.wait_send)
    for h in range(2):
        pl.when(s < last - 1)(up_copy(h).wait_send)
    for i in range(1, ndp):
        x_copy(i).wait_send()
    for i in range(1, ndp // 2):
        r_copy(i).wait_send()
    r_swap(plane).wait_send()

    def drain(m, carry):
        pl.when(ahead)(dr_copy(m).wait_send)

        @pl.when(s > 0)
        def _():
            for k in range(nchunk):
                chunk_copy(m, k).wait_send()

        @pl.when(node)
        def _():
            dr_pass(m).wait_send()
            for k in range(nchunk):
                pass_on(m, k).wait_send()

        for i in range(1, ndp // 2):
            q_copy(m, i).wait_send()
        q_swap(m, plane).wait_send()
        for i in range(1, ndp):
            y_copy(m, i).wait_send()
        return carry

    lax.fori_loop(0, micro, drain, 0)
    for copy in writes:
        copy.wait()
    out1.wait()
    out2.wait()


def shards(acts, out_grad, w_in, w_out, decay_rate, cycle_order):
    nsec = lax.axis_size("section")
    ndp = lax.axis_size("dp")
    _, micro, tok, width = acts.shape
    cols = w_out.shape[2]
    heads = decay_rate.shape[1]
    hd = cols // heads
    blk = width // ndp
    nchunk = 4
    dims = (nsec, ndp, micro, tok, width, heads, hd, nchunk)
    dma = pltpu.SemaphoreType.DMA
    any_spec = pl.BlockSpec(memory_space=pl.ANY)
    smem = pl.BlockSpec(memory_space=pltpu.SMEM)
    return pl.pallas_call(
        functools.partial(kernel, dims),
        name="retention_stack_back",
        out_shape=(
            jax.ShapeDtypeStruct((1, micro, tok, width), BF),
            jax.ShapeDtypeStruct((1, blk, 3 * cols), F32),
            jax.ShapeDtypeStruct((1, blk, cols), F32),
        ),
        in_specs=[any_spec] * 4 + [smem] * 2,
        out_specs=[any_spec] * 3,
        scratch_shapes=[
            pltpu.VMEM((ndp, blk, 3 * cols), BF),
            pltpu.VMEM((ndp, blk, cols), BF),
            pltpu.VMEM((ndp, blk, cols), BF),
            pltpu.VMEM((ndp, 3 * cols, blk), BF),
            pltpu.VMEM((3 * cols, cols), F32),
            pltpu.VMEM((3 * cols, cols), BF),
            pltpu.VMEM((micro, tok, cols), BF),
            pltpu.VMEM((micro, tok, cols), BF),
            pltpu.VMEM((micro, tok, cols), BF),
            pltpu.VMEM((tok, cols), F32),
            pltpu.VMEM((ndp, micro, tok, blk), BF),
            pltpu.VMEM((micro, ndp, tok, blk), BF),
            pltpu.VMEM((micro, ndp, tok, blk), BF),
            pltpu.VMEM((micro, ndp, tok, blk), BF),
            pltpu.VMEM((micro * tok, 3 * cols), F32),
            pltpu.VMEM((micro, tok, 3 * cols), BF),
            pltpu.VMEM((micro, heads, tok, tok), BF),
            pltpu.VMEM((heads, tok, tok), F32),
            pltpu.VMEM((micro, ndp * tok, blk), BF),
            pltpu.VMEM((micro, ndp * tok, blk), BF),
            pltpu.VMEM((micro, ndp * tok, 3 * cols), BF),
            pltpu.VMEM((micro, ndp * tok, cols), BF),
            pltpu.VMEM((blk, 3 * cols), F32),
            pltpu.VMEM((blk, cols), F32),
            dma((4 + ndp,)),
            dma((96,)),
            dma((ndp, 2, 3)),
            dma((micro, nchunk)),
            dma((micro, nchunk)),
            dma((micro, nchunk)),
            dma((micro, nchunk)),
            dma((micro,)),
            dma((micro,)),
            dma((micro,)),
            dma((micro,)),
            dma((ndp,)),
            dma((ndp,)),
            dma((ndp // 2,)),
            dma((ndp // 2,)),
            dma((micro, ndp // 2)),
            dma((micro, ndp // 2)),
            dma((micro, ndp)),
            dma((micro, ndp)),
            dma((ndp,)),
        ],
        compiler_params=pltpu.CompilerParams(
            collective_id=0, has_side_effects=True, vmem_limit_bytes=60 * 1024 * 1024
        ),
        cost_estimate=pl.CostEstimate(
            flops=6_000_000_000, bytes_accessed=8_000_000, transcendentals=4096
        ),
    )(acts, out_grad, w_in, w_out, decay_rate, cycle_order)


def solution(mesh):
    placed = (
        P("section", None, "dp", None),
        P(None, "dp", None),
        P("section", "dp", None),
        P("section", "dp", None),
        P("section", None),
        P(),
    )
    return jax.shard_map(
        shards,
        mesh=mesh,
        in_specs=placed,
        out_specs=(
            P("section", None, "dp", None),
            P("section", "dp", None),
            P("section", "dp", None),
        ),
        check_vma=False,
    )
```

```python
import functools

import jax
import jax.numpy as jnp
from jax import lax
from jax.experimental import pallas as pl
from jax.experimental.pallas import tpu as pltpu
from jax.sharding import PartitionSpec as P

MESH = pl.DeviceIdType.MESH
BF = jnp.bfloat16
F32 = jnp.float32


def dot(a, b):
    return jnp.dot(a, b, preferred_element_type=F32)


def dot_nt(a, b):
    return lax.dot_general(a, b, (((1,), (1,)), ((), ())), preferred_element_type=F32)


def dot_tn(a, b):
    return lax.dot_general(a, b, (((0,), (0,)), ((), ())), preferred_element_type=F32)


def kernel(
    dims,
    acts, out_grad, w_in, w_out, rates, order,
    in_grad, grad_in, grad_out,
    WI, WS, WO, WT, MA, MM, DRB, DRN, RD, XB, DY, NX, RB, ACC, QKV, SC, TAB, XS, DS, DQ, RA, GI, GO,
    loc, wsend, wrecv, csend, crecv, bsend, brecv, dsend, drecv, esend, erecv, xsend, xrecv, rsend, rrecv, qsend, qrecv, ysend, yrecv, outsem,
):
    nsec, ndp, micro, tok, width, heads, hd, nchunk = dims
    cols = heads * hd
    blk = width // ndp
    half = blk // 2
    per = ndp // nchunk
    nx = ndp // 4
    s = lax.axis_index("section")
    r = lax.axis_index("dp")
    x, zl, c = r // 4, (r // 2) % 2, r % 2
    last = nsec - 1
    lead = min(4, nsec // 4)
    ny = 4 if nsec >= 16 else 2
    y = lax.rem(s, ny)
    first = last - 2
    direct = s >= first
    ahead = (s > 0) & (s <= first)
    to_relay = (s > 0) & (y == 0) & (zl == 0)
    to_next = (s > 0) & ((y != 0) | (zl != 0))
    node = (s >= ny) & (y == ny - 1) & (zl == 0)
    by_relay = (s < last) & (y == ny - 1) & (zl == 0)
    by_prev = (s < last) & ((y != ny - 1) | (zl != 0))
    slot = c * (ndp // 2) + r // 2

    def rep(xx, zz, cc):
        return lax.rem(xx + nx, nx) * 4 + zz * 2 + cc

    core, zp = rep(x, zl, 1 - c), rep(x, 1 - zl, c)
    xp, xm, xo = rep(x + 1, zl, c), rep(x - 1, zl, c), rep(x + 2, zl, c)
    xpz, xmz, xoz = rep(x + 1, 1 - zl, c), rep(x - 1, 1 - zl, c), rep(x + 2, 1 - zl, c)

    def peer(i):
        return lax.rem(r + i, ndp)

    def slot_of(q):
        return lax.rem(q, 2) * (ndp // 2) + q // 2

    local = [
        pltpu.make_async_copy(w_in.at[0], WI.at[r], loc.at[0]),
        pltpu.make_async_copy(w_out.at[0], WS.at[r], loc.at[1]),
    ]
    for i in range(ndp):
        local.append(
            pltpu.make_async_copy(
                acts.at[0, :, :, pl.ds(i * blk, blk)], XB.at[i], loc.at[2 + i]
            )
        )
    for copy in local:
        copy.start()

    barrier = pltpu.get_barrier_semaphore()
    for i in range(1, ndp):
        pl.semaphore_signal(barrier, inc=1, device_id=(s, peer(i)), device_id_type=MESH)

    def greet(cond, section):
        @pl.when(cond)
        def _():
            pl.semaphore_signal(
                barrier, inc=1, device_id=(section, r), device_id_type=MESH
            )

    greet(by_prev, jnp.minimum(s + 1, last))
    greet(by_relay, jnp.minimum(s + ny, last))
    greet(node, jnp.maximum(s - (ny - 1), 0))
    greet(ahead, jnp.maximum(s - 1, 0))
    receivers = (
        jnp.where(to_next, 1, 0)
        + jnp.where(to_relay, 1, 0)
        + jnp.where(node, 1, 0)
        + jnp.where(s < first, 1, 0)
    )
    pl.semaphore_wait(barrier, ndp - 1 + receivers)

    def piece(ref, q, h):
        return ref.at[q, pl.ds(h * half, half)]

    sent = []
    needed = (s >= 0, direct, ahead)

    def push(q, h, target, arrays=(0, 1, 2), own=False):
        for which in arrays:
            ref = (WI, WS, WO)[which]
            src = piece(ref, q, h)
            if own and which < 2:
                src = (w_in, w_out)[which].at[0, pl.ds(h * half, half)]
            copy = pltpu.make_async_remote_copy(
                src_ref=src,
                dst_ref=piece(ref, q, h),
                send_sem=wsend.at[len(sent)],
                recv_sem=wrecv.at[q, h, which],
                device_id=(s, target),
                device_id_type=MESH,
            )
            sent.append((copy, needed[which]))
            pl.when(needed[which])(copy.start)

    def arrive(q, h):
        for which, ref in enumerate((WI, WS, WO)):
            copy = pltpu.make_async_remote_copy(
                src_ref=piece(ref, q, h),
                dst_ref=piece(ref, q, h),
                send_sem=wsend.at[0],
                recv_sem=wrecv.at[q, h, which],
                device_id=(s, core),
                device_id_type=MESH,
            )
            pl.when(needed[which])(copy.wait_recv)

    def up_copy(h):
        return pltpu.make_async_remote_copy(
            src_ref=w_out.at[0, pl.ds(h * half, half)],
            dst_ref=piece(WO, r, h),
            send_sem=loc.at[2 + ndp + h],
            recv_sem=wrecv.at[r, h, 2],
            device_id=(jnp.minimum(s + 1, last), r),
            device_id_type=MESH,
        )

    for h in range(2):
        pl.when(s < first)(up_copy(h).start)
    for h in range(2):
        for target in (xp, xm, zp, core):
            push(r, h, target, arrays=(0, 1), own=True)

    MA[...] = jnp.zeros_like(MA)
    ACC[...] = jnp.zeros_like(ACC)

    def fold(q):
        MA[...] += dot(WT[q], WO[q])

    def add(q):
        ACC[...] += dot(XB[q].reshape(micro * tok, blk), WI[q])
        WT[q] = WI[q].T
        pl.when(ahead)(functools.partial(fold, q))

    for copy in local:
        copy.wait()

    @pl.when(s == last)
    def _():
        for i in range(ndp):
            pltpu.make_async_copy(
                out_grad.at[:, :, pl.ds(i * blk, blk)], DY.at[:, i], outsem.at[i]
            ).start()

    spot_t = lax.broadcasted_iota(jnp.int32, (tok, tok), 0)
    spot_j = lax.broadcasted_iota(jnp.int32, (tok, tok), 1)
    offset = (spot_t - spot_j).astype(F32)
    for h in range(heads):
        decayed = jnp.exp(-rates[0, h] * jnp.maximum(offset, 0.0))
        TAB[h] = jnp.where(offset >= 0.0, decayed, 0.0)

    @pl.when(ahead)
    def _():
        for h in range(2):
            up_copy(h).wait_recv()

    for h in range(2):
        for target in (xp, xm, zp, core):
            push(r, h, target, arrays=(2,))
    add(r)
    arrive(xm, 0)
    push(xm, 0, xp)
    push(xm, 0, core)
    arrive(xp, 0)
    push(xp, 0, core)
    arrive(zp, 0)
    push(zp, 0, xp)
    push(zp, 0, xm)
    push(zp, 0, core)
    arrive(core, 0)
    arrive(core, 1)
    add(core)
    arrive(xp, 1)
    push(xp, 1, xm)
    push(xp, 1, core)
    arrive(xm, 1)
    push(xm, 1, core)
    arrive(zp, 1)
    push(zp, 1, xp)
    push(zp, 1, xm)
    push(zp, 1, core)
    add(xm)
    add(xp)
    add(zp)
    arrive(xo, 0)
    push(xo, 0, zp)
    push(xo, 0, core)
    arrive(xo, 1)
    push(xo, 1, zp)
    push(xo, 1, core)

    def other(q):
        return q + 1 - 2 * c

    for q in (xm, xp, zp):
        arrive(other(q), 0)
        arrive(other(q), 1)
        add(other(q))
    add(xo)
    for q in (xmz, xpz):
        for h in range(2):
            arrive(q, h)
            push(q, h, core)
    arrive(xoz, 0)
    push(xoz, 0, core)
    add(xmz)
    add(xpz)
    arrive(xoz, 1)
    push(xoz, 1, core)
    for q in (xo, xmz, xpz):
        arrive(other(q), 0)
        arrive(other(q), 1)
        add(other(q))
    add(xoz)
    arrive(other(xoz), 0)
    arrive(other(xoz), 1)
    add(other(xoz))

    MM[...] = MA[...].astype(BF)
    failed = order[ndp - 1]
    live = jnp.where(r == failed, 0.0, 1.0).astype(F32)
    mine = pl.ds(pl.multiple_of(slot * tok, tok), tok)

    QKV[...] = ACC[...].astype(BF).reshape(micro, tok, 3 * cols)
    for m in range(micro):
        for h in range(heads):
            q = QKV[m, :, h * hd : (h + 1) * hd]
            k = QKV[m, :, cols + h * hd : cols + (h + 1) * hd]
            v = QKV[m, :, 2 * cols + h * hd : 2 * cols + (h + 1) * hd]
            score = (dot_nt(q, k) * TAB[h] / hd).astype(BF)
            SC[m, h] = score
            mixed = dot(score, v).astype(BF)
            RA[m, mine, h * hd : (h + 1) * hd] = (mixed.astype(F32) * live).astype(BF)

    plane = pl.ds(pl.multiple_of(c * (ndp // 2) * tok, tok), (ndp // 2) * tok)
    foreign = pl.ds(pl.multiple_of((1 - c) * (ndp // 2) * tok, tok), (ndp // 2) * tok)

    def rows_of(q):
        return pl.ds(pl.multiple_of(slot_of(q) * tok, tok), tok)

    def x_copy(i):
        q = peer(i)
        return pltpu.make_async_remote_copy(
            src_ref=XB.at[q], dst_ref=XS.at[:, mine],
            send_sem=xsend.at[i], recv_sem=xrecv.at[i],
            device_id=(s, q), device_id_type=MESH,
        )

    def x_wait(i):
        q = lax.rem(r - i + ndp, ndp)
        pltpu.make_async_remote_copy(
            src_ref=XB.at[q], dst_ref=XS.at[:, rows_of(q)],
            send_sem=xsend.at[i], recv_sem=xrecv.at[i],
            device_id=(s, q), device_id_type=MESH,
        ).wait_recv()

    def r_copy(i):
        q = peer(2 * i)
        return pltpu.make_async_remote_copy(
            src_ref=RA.at[:, mine], dst_ref=RA.at[:, mine],
            send_sem=rsend.at[i], recv_sem=rrecv.at[i],
            device_id=(s, q), device_id_type=MESH,
        )

    def r_wait(i):
        q = lax.rem(r - 2 * i + ndp, ndp)
        pltpu.make_async_remote_copy(
            src_ref=RA.at[:, rows_of(q)], dst_ref=RA.at[:, rows_of(q)],
            send_sem=rsend.at[i], recv_sem=rrecv.at[i],
            device_id=(s, q), device_id_type=MESH,
        ).wait_recv()

    def r_swap(rows):
        return pltpu.make_async_remote_copy(
            src_ref=RA.at[:, rows], dst_ref=RA.at[:, rows],
            send_sem=rsend.at[0], recv_sem=rrecv.at[0],
            device_id=(s, core), device_id_type=MESH,
        )

    own_x = pltpu.make_async_copy(XB.at[r], XS.at[:, mine], loc.at[0])

    def exchange_early():
        for i in range(1, ndp // 2):
            r_copy(i).start()
        own_x.start()
        for i in range(1, ndp):
            x_copy(i).start()
        for i in range(1, ndp // 2):
            r_wait(i)
        r_swap(plane).start()
        own_x.wait()
        for i in range(1, ndp):
            x_wait(i)
        r_swap(foreign).wait_recv()

    GI[...] = jnp.zeros_like(GI)
    GO[...] = jnp.zeros_like(GO)
    early = s < last - lead
    pl.when(early)(exchange_early)

    def chunk_copy(m, k):
        part = pl.ds(k * per, per)
        return pltpu.make_async_remote_copy(
            src_ref=NX.at[m, part], dst_ref=DY.at[m, part],
            send_sem=csend.at[m, k], recv_sem=crecv.at[m, k],
            device_id=(jnp.maximum(s - 1, 0), r), device_id_type=MESH,
        )

    def relay_copy(m, k):
        part = pl.ds(k * per, per)
        return pltpu.make_async_remote_copy(
            src_ref=NX.at[m, part], dst_ref=RB.at[m, part],
            send_sem=csend.at[m, k], recv_sem=brecv.at[m, k],
            device_id=(jnp.minimum(s + ny - 1, last), r), device_id_type=MESH,
        )

    def pass_on(m, k):
        part = pl.ds(k * per, per)
        return pltpu.make_async_remote_copy(
            src_ref=RB.at[m, part], dst_ref=DY.at[m, part],
            send_sem=bsend.at[m, k], recv_sem=crecv.at[m, k],
            device_id=(jnp.maximum(s - ny, 0), r), device_id_type=MESH,
        )

    def dr_copy(m):
        return pltpu.make_async_remote_copy(
            src_ref=DRN.at[m], dst_ref=DRB.at[m],
            send_sem=dsend.at[m], recv_sem=drecv.at[m],
            device_id=(jnp.maximum(s - 1, 0), r), device_id_type=MESH,
        )

    def dr_relay(m):
        return pltpu.make_async_remote_copy(
            src_ref=DRN.at[m], dst_ref=RD.at[m],
            send_sem=dsend.at[m], recv_sem=erecv.at[m],
            device_id=(jnp.minimum(s + ny - 1, last), r), device_id_type=MESH,
        )

    def dr_pass(m):
        return pltpu.make_async_remote_copy(
            src_ref=RD.at[m], dst_ref=DRB.at[m],
            send_sem=esend.at[m], recv_sem=drecv.at[m],
            device_id=(jnp.maximum(s - ny, 0), r), device_id_type=MESH,
        )

    def q_copy(m, i):
        q = peer(2 * i)
        return pltpu.make_async_remote_copy(
            src_ref=DQ.at[m, mine], dst_ref=DQ.at[m, mine],
            send_sem=qsend.at[m, i], recv_sem=qrecv.at[m, i],
            device_id=(s, q), device_id_type=MESH,
        )

    def q_wait(m, i):
        q = lax.rem(r - 2 * i + ndp, ndp)
        pltpu.make_async_remote_copy(
            src_ref=DQ.at[m, rows_of(q)], dst_ref=DQ.at[m, rows_of(q)],
            send_sem=qsend.at[m, i], recv_sem=qrecv.at[m, i],
            device_id=(s, q), device_id_type=MESH,
        ).wait_recv()

    def q_swap(m, rows):
        return pltpu.make_async_remote_copy(
            src_ref=DQ.at[m, rows], dst_ref=DQ.at[m, rows],
            send_sem=qsend.at[m, 0], recv_sem=qrecv.at[m, 0],
            device_id=(s, core), device_id_type=MESH,
        )

    def both(q):
        return pl.ds(2 * (q // 2), 2)

    def y_copy(m, i):
        q = peer(2 * i)
        return pltpu.make_async_remote_copy(
            src_ref=DY.at[m, both(q)], dst_ref=DS.at[m, :, mine],
            send_sem=ysend.at[m, i], recv_sem=yrecv.at[m, i],
            device_id=(s, q), device_id_type=MESH,
        )

    def y_wait(m, i):
        q = lax.rem(r - 2 * i + ndp, ndp)
        pltpu.make_async_remote_copy(
            src_ref=DY.at[m, both(q)], dst_ref=DS.at[m, :, rows_of(q)],
            send_sem=ysend.at[m, i], recv_sem=yrecv.at[m, i],
            device_id=(s, q), device_id_type=MESH,
        ).wait_recv()

    def y_swap(m, which, rows):
        return pltpu.make_async_remote_copy(
            src_ref=DS.at[m, which, rows], dst_ref=DS.at[m, which, rows],
            send_sem=ysend.at[m, 0], recv_sem=yrecv.at[m, 0],
            device_id=(s, core), device_id_type=MESH,
        )

    @pl.when(s == last)
    def _():
        for i in range(ndp):
            pltpu.make_async_copy(
                out_grad.at[:, :, pl.ds(i * blk, blk)], DY.at[:, i], outsem.at[i]
            ).wait()

    def settle(m):
        q_swap(m, foreign).wait_recv()
        y_swap(m, c, foreign).wait_recv()
        GI[...] += dot_tn(XS[m], DQ[m])
        GO[...] += dot_tn(DS[m, c], RA[m])

    def exchange(m):
        for i in range(1, ndp // 2):
            q_copy(m, i).start()
        for i in range(1, ndp // 2):
            y_copy(m, i).start()

    inline = s < nsec // 4

    def step(m, carry):
        @pl.when(direct)
        def _():
            for k in range(nchunk):
                pl.when(s < last)(chunk_copy(m, k).wait_recv)
            rows = jnp.concatenate([DY[m, j] for j in range(ndp)], axis=1)
            DRB[m] = dot(rows, WS[...].reshape(width, cols)).astype(BF)

        pl.when(s < first)(dr_copy(m).wait_recv)
        d_mixed = DRB[m]
        parts = [[], [], []]
        for h in range(heads):
            q = QKV[m, :, h * hd : (h + 1) * hd]
            k = QKV[m, :, cols + h * hd : cols + (h + 1) * hd]
            v = QKV[m, :, 2 * cols + h * hd : 2 * cols + (h + 1) * hd]
            dr = d_mixed[:, h * hd : (h + 1) * hd]
            d_score = (dot_nt(dr, v) * TAB[h] / hd).astype(BF)
            parts[0].append(dot(d_score, k).astype(BF))
            parts[1].append(dot_tn(d_score, q).astype(BF))
            parts[2].append(dot_tn(SC[m, h], dr).astype(BF))
        d_all = jnp.concatenate(parts[0] + parts[1] + parts[2], axis=1)

        total = dot(d_all, MM[...])
        for k in range(nchunk):
            pl.when(s < first)(chunk_copy(m, k).wait_recv)
            span = range(k * per, (k + 1) * per)
            rows = jnp.concatenate([DY[m, j] for j in span], axis=1)
            total += dot(rows, WO[k * per : (k + 1) * per].reshape(per * blk, cols))
            if k == nchunk - 1:
                DRN[m] = total.astype(BF)
                pl.when(ahead & to_next)(dr_copy(m).start)
                pl.when(ahead & to_relay)(dr_relay(m).start)
            for j in span:
                back = dot(d_all, WT[j])
                NX[m, j] = (DY[m, j].astype(F32) + back).astype(BF)

            @pl.when(to_next)
            def _():
                chunk_copy(m, k).start()

            @pl.when(to_relay)
            def _():
                relay_copy(m, k).start()

        DQ[m, mine] = (d_all.astype(F32) * live).astype(BF)
        DS[m, :, mine] = DY[m, both(r)]

        @pl.when(inline)
        def _():
            exchange(m)

        return carry

    lax.fori_loop(0, micro, step, 0)
    writes = [
        pltpu.make_async_copy(
            NX.at[:, i], in_grad.at[0, :, :, pl.ds(i * blk, blk)], outsem.at[i]
        )
        for i in range(ndp)
    ]
    for copy in writes:
        copy.start()

    @pl.when(node)
    def _():
        def forward(m, carry):
            for k in range(nchunk):
                if k == nchunk - 1:
                    dr_relay(m).wait_recv()
                    dr_pass(m).start()
                relay_copy(m, k).wait_recv()
                pass_on(m, k).start()
            return carry

        lax.fori_loop(0, micro, forward, 0)

    pl.when(s >= last - lead)(exchange_early)

    @pl.when(s >= nsec // 4)
    def _():
        def send(m, carry):
            exchange(m)
            return carry

        lax.fori_loop(0, micro, send, 0)

    scale = 1.0 / (ndp - 1.0)

    def swap(m):
        for i in range(1, ndp // 2):
            q_wait(m, i)
        q_swap(m, plane).start()
        for i in range(1, ndp // 2):
            y_wait(m, i)
        y_swap(m, 1 - c, plane).start()

    swap(0)

    def finish(m, carry):
        swap(m + 1)
        settle(m)
        return carry

    lax.fori_loop(0, micro - 1, finish, 0)
    m = micro - 1
    y_swap(m, c, foreign).wait_recv()
    GO[...] = (GO[...] + dot_tn(DS[m, c], RA[m])) * scale
    out1 = pltpu.make_async_copy(GO, grad_out.at[0], loc.at[1])
    out1.start()
    q_swap(m, foreign).wait_recv()
    GI[...] = (GI[...] + dot_tn(XS[m], DQ[m])) * scale
    out2 = pltpu.make_async_copy(GI, grad_in.at[0], loc.at[2])
    out2.start()

    for copy, cond in sent:
        pl.when(cond)(copy.wait_send)
    for h in range(2):
        pl.when(s < first)(up_copy(h).wait_send)
    for i in range(1, ndp):
        x_copy(i).wait_send()
    for i in range(1, ndp // 2):
        r_copy(i).wait_send()
    r_swap(plane).wait_send()

    def drain(m, carry):
        pl.when(ahead)(dr_copy(m).wait_send)

        @pl.when(s > 0)
        def _():
            for k in range(nchunk):
                chunk_copy(m, k).wait_send()

        @pl.when(node)
        def _():
            dr_pass(m).wait_send()
            for k in range(nchunk):
                pass_on(m, k).wait_send()

        for i in range(1, ndp // 2):
            q_copy(m, i).wait_send()
        q_swap(m, plane).wait_send()
        for i in range(1, ndp // 2):
            y_copy(m, i).wait_send()
        y_swap(m, 1 - c, plane).wait_send()
        return carry

    lax.fori_loop(0, micro, drain, 0)
    for copy in writes:
        copy.wait()
    out1.wait()
    out2.wait()


def shards(acts, out_grad, w_in, w_out, decay_rate, cycle_order):
    nsec = lax.axis_size("section")
    ndp = lax.axis_size("dp")
    _, micro, tok, width = acts.shape
    cols = w_out.shape[2]
    heads = decay_rate.shape[1]
    hd = cols // heads
    blk = width // ndp
    nchunk = 2
    dims = (nsec, ndp, micro, tok, width, heads, hd, nchunk)
    dma = pltpu.SemaphoreType.DMA
    any_spec = pl.BlockSpec(memory_space=pl.ANY)
    smem = pl.BlockSpec(memory_space=pltpu.SMEM)
    return pl.pallas_call(
        functools.partial(kernel, dims),
        name="retention_stack_back",
        out_shape=(
            jax.ShapeDtypeStruct((1, micro, tok, width), BF),
            jax.ShapeDtypeStruct((1, blk, 3 * cols), F32),
            jax.ShapeDtypeStruct((1, blk, cols), F32),
        ),
        in_specs=[any_spec] * 4 + [smem] * 2,
        out_specs=[any_spec] * 3,
        scratch_shapes=[
            pltpu.VMEM((ndp, blk, 3 * cols), BF),
            pltpu.VMEM((ndp, blk, cols), BF),
            pltpu.VMEM((ndp, blk, cols), BF),
            pltpu.VMEM((ndp, 3 * cols, blk), BF),
            pltpu.VMEM((3 * cols, cols), F32),
            pltpu.VMEM((3 * cols, cols), BF),
            pltpu.VMEM((micro, tok, cols), BF),
            pltpu.VMEM((micro, tok, cols), BF),
            pltpu.VMEM((micro, tok, cols), BF),
            pltpu.VMEM((ndp, micro, tok, blk), BF),
            pltpu.VMEM((micro, ndp, tok, blk), BF),
            pltpu.VMEM((micro, ndp, tok, blk), BF),
            pltpu.VMEM((micro, ndp, tok, blk), BF),
            pltpu.VMEM((micro * tok, 3 * cols), F32),
            pltpu.VMEM((micro, tok, 3 * cols), BF),
            pltpu.VMEM((micro, heads, tok, tok), BF),
            pltpu.VMEM((heads, tok, tok), F32),
            pltpu.VMEM((micro, ndp * tok, blk), BF),
            pltpu.VMEM((micro, 2, ndp * tok, blk), BF),
            pltpu.VMEM((micro, ndp * tok, 3 * cols), BF),
            pltpu.VMEM((micro, ndp * tok, cols), BF),
            pltpu.VMEM((blk, 3 * cols), F32),
            pltpu.VMEM((blk, cols), F32),
            dma((4 + ndp,)),
            dma((96,)),
            dma((ndp, 2, 3)),
            dma((micro, nchunk)),
            dma((micro, nchunk)),
            dma((micro, nchunk)),
            dma((micro, nchunk)),
            dma((micro,)),
            dma((micro,)),
            dma((micro,)),
            dma((micro,)),
            dma((ndp,)),
            dma((ndp,)),
            dma((ndp // 2,)),
            dma((ndp // 2,)),
            dma((micro, ndp // 2)),
            dma((micro, ndp // 2)),
            dma((micro, ndp // 2)),
            dma((micro, ndp // 2)),
            dma((ndp,)),
        ],
        compiler_params=pltpu.CompilerParams(
            collective_id=0, has_side_effects=True, vmem_limit_bytes=60 * 1024 * 1024
        ),
        cost_estimate=pl.CostEstimate(
            flops=6_000_000_000, bytes_accessed=8_000_000, transcendentals=4096
        ),
    )(acts, out_grad, w_in, w_out, decay_rate, cycle_order)


def solution(mesh):
    placed = (
        P("section", None, "dp", None),
        P(None, "dp", None),
        P("section", "dp", None),
        P("section", "dp", None),
        P("section", None),
        P(),
    )
    return jax.shard_map(
        shards,
        mesh=mesh,
        in_specs=placed,
        out_specs=(
            P("section", None, "dp", None),
            P("section", "dp", None),
            P("section", "dp", None),
        ),
        check_vma=False,
    )
```

```python
import functools

import jax
import jax.numpy as jnp
from jax import lax
from jax.experimental import pallas as pl
from jax.experimental.pallas import tpu as pltpu
from jax.sharding import PartitionSpec as P

MESH = pl.DeviceIdType.MESH
BF = jnp.bfloat16
F32 = jnp.float32


def dot(a, b):
    return jnp.dot(a, b, preferred_element_type=F32)


def dot_nt(a, b):
    return lax.dot_general(a, b, (((1,), (1,)), ((), ())), preferred_element_type=F32)


def dot_tn(a, b):
    return lax.dot_general(a, b, (((0,), (0,)), ((), ())), preferred_element_type=F32)


def kernel(
    dims,
    acts, out_grad, w_in, w_out, rates, order,
    in_grad, grad_in, grad_out,
    WI, WS, WO, WT, MA, MM, DRB, DRN, RD, XB, DY, NX, RB, ACC, QKV, SC, TAB, XS, DS, DQ, RA, GI, GO,
    loc, wsend, wrecv, csend, crecv, bsend, brecv, dsend, drecv, esend, erecv, xsend, xrecv, rsend, rrecv, qsend, qrecv, ysend, yrecv, outsem,
):
    nsec, ndp, micro, tok, width, heads, hd, nchunk = dims
    cols = heads * hd
    blk = width // ndp
    half = blk // 2
    per = ndp // nchunk
    nx = ndp // 4
    s = lax.axis_index("section")
    r = lax.axis_index("dp")
    x, zl, c = r // 4, (r // 2) % 2, r % 2
    last = nsec - 1
    lead = min(4, nsec // 4)
    ny = 4 if nsec >= 16 else 2
    y = lax.rem(s, ny)
    first = last - 2
    direct = s >= first
    ahead = (s > 0) & (s <= first)
    to_relay = (s > 0) & (y == 0) & (zl == 0)
    to_next = (s > 0) & ((y != 0) | (zl != 0))
    node = (s >= ny) & (y == ny - 1) & (zl == 0)
    by_relay = (s < last) & (y == ny - 1) & (zl == 0)
    by_prev = (s < last) & ((y != ny - 1) | (zl != 0))
    slot = c * (ndp // 2) + r // 2

    def rep(xx, zz, cc):
        return lax.rem(xx + nx, nx) * 4 + zz * 2 + cc

    core, zp = rep(x, zl, 1 - c), rep(x, 1 - zl, c)
    xp, xm, xo = rep(x + 1, zl, c), rep(x - 1, zl, c), rep(x + 2, zl, c)
    xpz, xmz, xoz = rep(x + 1, 1 - zl, c), rep(x - 1, 1 - zl, c), rep(x + 2, 1 - zl, c)

    def peer(i):
        return lax.rem(r + i, ndp)

    def slot_of(q):
        return lax.rem(q, 2) * (ndp // 2) + q // 2

    local = [
        pltpu.make_async_copy(w_in.at[0], WI.at[r], loc.at[0]),
        pltpu.make_async_copy(w_out.at[0], WS.at[r], loc.at[1]),
    ]
    for i in range(ndp):
        local.append(
            pltpu.make_async_copy(
                acts.at[0, :, :, pl.ds(i * blk, blk)], XB.at[i], loc.at[2 + i]
            )
        )
    for copy in local:
        copy.start()

    barrier = pltpu.get_barrier_semaphore()
    for i in range(1, ndp):
        pl.semaphore_signal(barrier, inc=1, device_id=(s, peer(i)), device_id_type=MESH)

    def greet(cond, section):
        @pl.when(cond)
        def _():
            pl.semaphore_signal(
                barrier, inc=1, device_id=(section, r), device_id_type=MESH
            )

    greet(by_prev, jnp.minimum(s + 1, last))
    greet(by_relay, jnp.minimum(s + ny, last))
    greet(node, jnp.maximum(s - (ny - 1), 0))
    greet(ahead, jnp.maximum(s - 1, 0))
    receivers = (
        jnp.where(to_next, 1, 0)
        + jnp.where(to_relay, 1, 0)
        + jnp.where(node, 1, 0)
        + jnp.where(s < first, 1, 0)
    )
    pl.semaphore_wait(barrier, ndp - 1 + receivers)

    def piece(ref, q, h):
        return ref.at[q, pl.ds(h * half, half)]

    sent = []
    needed = (s >= 0, direct, ahead)

    def push(q, h, target, arrays=(0, 1, 2), own=False):
        for which in arrays:
            ref = (WI, WS, WO)[which]
            src = piece(ref, q, h)
            if own and which < 2:
                src = (w_in, w_out)[which].at[0, pl.ds(h * half, half)]
            copy = pltpu.make_async_remote_copy(
                src_ref=src,
                dst_ref=piece(ref, q, h),
                send_sem=wsend.at[len(sent)],
                recv_sem=wrecv.at[q, h, which],
                device_id=(s, target),
                device_id_type=MESH,
            )
            sent.append((copy, needed[which]))
            pl.when(needed[which])(copy.start)

    def arrive(q, h):
        for which, ref in enumerate((WI, WS, WO)):
            copy = pltpu.make_async_remote_copy(
                src_ref=piece(ref, q, h),
                dst_ref=piece(ref, q, h),
                send_sem=wsend.at[0],
                recv_sem=wrecv.at[q, h, which],
                device_id=(s, core),
                device_id_type=MESH,
            )
            pl.when(needed[which])(copy.wait_recv)

    def up_copy(h):
        return pltpu.make_async_remote_copy(
            src_ref=w_out.at[0, pl.ds(h * half, half)],
            dst_ref=piece(WO, r, h),
            send_sem=loc.at[2 + ndp + h],
            recv_sem=wrecv.at[r, h, 2],
            device_id=(jnp.minimum(s + 1, last), r),
            device_id_type=MESH,
        )

    for h in range(2):
        pl.when(s < first)(up_copy(h).start)
    for h in range(2):
        for target in (xp, xm, zp, core):
            push(r, h, target, arrays=(0, 1), own=True)

    MA[...] = jnp.zeros_like(MA)
    ACC[...] = jnp.zeros_like(ACC)

    def fold(q):
        MA[...] += dot(WT[q], WO[q])

    def add(q):
        ACC[...] += dot(XB[q].reshape(micro * tok, blk), WI[q])
        WT[q] = WI[q].T
        pl.when(ahead)(functools.partial(fold, q))

    for copy in local:
        copy.wait()

    @pl.when(s == last)
    def _():
        for i in range(ndp):
            pltpu.make_async_copy(
                out_grad.at[:, :, pl.ds(i * blk, blk)], DY.at[:, i], outsem.at[i]
            ).start()

    spot_t = lax.broadcasted_iota(jnp.int32, (tok, tok), 0)
    spot_j = lax.broadcasted_iota(jnp.int32, (tok, tok), 1)
    offset = (spot_t - spot_j).astype(F32)
    for h in range(heads):
        decayed = jnp.exp(-rates[0, h] * jnp.maximum(offset, 0.0))
        TAB[h] = jnp.where(offset >= 0.0, decayed, 0.0) / hd

    @pl.when(ahead)
    def _():
        for h in range(2):
            up_copy(h).wait_recv()

    for h in range(2):
        for target in (xp, xm, zp, core):
            push(r, h, target, arrays=(2,))
    add(r)
    arrive(xm, 0)
    push(xm, 0, xp)
    push(xm, 0, core)
    arrive(xp, 0)
    push(xp, 0, core)
    arrive(zp, 0)
    push(zp, 0, xp)
    push(zp, 0, xm)
    push(zp, 0, core)
    arrive(core, 0)
    arrive(core, 1)
    add(core)
    arrive(xp, 1)
    push(xp, 1, xm)
    push(xp, 1, core)
    arrive(xm, 1)
    push(xm, 1, core)
    arrive(zp, 1)
    push(zp, 1, xp)
    push(zp, 1, xm)
    push(zp, 1, core)
    add(xm)
    add(xp)
    add(zp)
    arrive(xo, 0)
    push(xo, 0, zp)
    push(xo, 0, core)
    arrive(xo, 1)
    push(xo, 1, zp)
    push(xo, 1, core)

    def other(q):
        return q + 1 - 2 * c

    for q in (xm, xp, zp):
        arrive(other(q), 0)
        arrive(other(q), 1)
        add(other(q))
    add(xo)
    for q in (xmz, xpz):
        for h in range(2):
            arrive(q, h)
            push(q, h, core)
    arrive(xoz, 0)
    push(xoz, 0, core)
    add(xmz)
    add(xpz)
    arrive(xoz, 1)
    push(xoz, 1, core)
    for q in (xo, xmz, xpz):
        arrive(other(q), 0)
        arrive(other(q), 1)
        add(other(q))
    add(xoz)
    arrive(other(xoz), 0)
    arrive(other(xoz), 1)
    add(other(xoz))

    @pl.when(ahead)
    def _():
        MM[...] = MA[...].astype(BF)

    failed = order[ndp - 1]
    live = jnp.where(r == failed, 0.0, 1.0).astype(F32)
    mine = pl.ds(pl.multiple_of(slot * tok, tok), tok)

    QKV[...] = ACC[...].astype(BF).reshape(micro, tok, 3 * cols)
    for m in range(micro):
        for h in range(heads):
            q = QKV[m, :, h * hd : (h + 1) * hd]
            k = QKV[m, :, cols + h * hd : cols + (h + 1) * hd]
            SC[m, h] = (dot_nt(q, k) * TAB[h]).astype(BF)

    plane = pl.ds(pl.multiple_of(c * (ndp // 2) * tok, tok), (ndp // 2) * tok)
    foreign = pl.ds(pl.multiple_of((1 - c) * (ndp // 2) * tok, tok), (ndp // 2) * tok)

    def rows_of(q):
        return pl.ds(pl.multiple_of(slot_of(q) * tok, tok), tok)

    def x_copy(i):
        q = peer(i)
        return pltpu.make_async_remote_copy(
            src_ref=XB.at[q], dst_ref=XS.at[:, mine],
            send_sem=xsend.at[i], recv_sem=xrecv.at[i],
            device_id=(s, q), device_id_type=MESH,
        )

    def x_wait(i):
        q = lax.rem(r - i + ndp, ndp)
        pltpu.make_async_remote_copy(
            src_ref=XB.at[q], dst_ref=XS.at[:, rows_of(q)],
            send_sem=xsend.at[i], recv_sem=xrecv.at[i],
            device_id=(s, q), device_id_type=MESH,
        ).wait_recv()

    def r_copy(i):
        q = peer(2 * i)
        return pltpu.make_async_remote_copy(
            src_ref=RA.at[:, mine], dst_ref=RA.at[:, mine],
            send_sem=rsend.at[i], recv_sem=rrecv.at[i],
            device_id=(s, q), device_id_type=MESH,
        )

    def r_wait(i):
        q = lax.rem(r - 2 * i + ndp, ndp)
        pltpu.make_async_remote_copy(
            src_ref=RA.at[:, rows_of(q)], dst_ref=RA.at[:, rows_of(q)],
            send_sem=rsend.at[i], recv_sem=rrecv.at[i],
            device_id=(s, q), device_id_type=MESH,
        ).wait_recv()

    def r_swap(rows):
        return pltpu.make_async_remote_copy(
            src_ref=RA.at[:, rows], dst_ref=RA.at[:, rows],
            send_sem=rsend.at[0], recv_sem=rrecv.at[0],
            device_id=(s, core), device_id_type=MESH,
        )

    own_x = pltpu.make_async_copy(XB.at[r], XS.at[:, mine], loc.at[0])

    def exchange_early():
        for m in range(micro):
            for h in range(heads):
                v = QKV[m, :, 2 * cols + h * hd : 2 * cols + (h + 1) * hd]
                mixed = dot(SC[m, h], v).astype(BF)
                RA[m, mine, h * hd : (h + 1) * hd] = (mixed.astype(F32) * live).astype(BF)
        for i in range(1, ndp // 2):
            r_copy(i).start()
        own_x.start()
        for i in range(1, ndp):
            x_copy(i).start()
        for i in range(1, ndp // 2):
            r_wait(i)
        r_swap(plane).start()
        own_x.wait()
        for i in range(1, ndp):
            x_wait(i)
        r_swap(foreign).wait_recv()
        for i in range(1, ndp):
            x_copy(i).wait_send()
        for i in range(1, ndp // 2):
            r_copy(i).wait_send()
        r_swap(plane).wait_send()
        for copy, cond in sent:
            pl.when(cond)(copy.wait_send)
        for h in range(2):
            pl.when(s < first)(up_copy(h).wait_send)

    GI[...] = jnp.zeros_like(GI)
    GO[...] = jnp.zeros_like(GO)
    early = s < last - lead
    pl.when(early)(exchange_early)

    def chunk_copy(m, k):
        part = pl.ds(k * per, per)
        return pltpu.make_async_remote_copy(
            src_ref=NX.at[m, part], dst_ref=DY.at[m, part],
            send_sem=csend.at[m, k], recv_sem=crecv.at[m, k],
            device_id=(jnp.maximum(s - 1, 0), r), device_id_type=MESH,
        )

    def relay_copy(m, k):
        part = pl.ds(k * per, per)
        return pltpu.make_async_remote_copy(
            src_ref=NX.at[m, part], dst_ref=RB.at[m, part],
            send_sem=csend.at[m, k], recv_sem=brecv.at[m, k],
            device_id=(jnp.minimum(s + ny - 1, last), r), device_id_type=MESH,
        )

    def pass_on(m, k):
        part = pl.ds(k * per, per)
        return pltpu.make_async_remote_copy(
            src_ref=RB.at[m, part], dst_ref=DY.at[m, part],
            send_sem=bsend.at[m, k], recv_sem=crecv.at[m, k],
            device_id=(jnp.maximum(s - ny, 0), r), device_id_type=MESH,
        )

    def dr_copy(m):
        return pltpu.make_async_remote_copy(
            src_ref=DRN.at[m], dst_ref=DRB.at[m],
            send_sem=dsend.at[m], recv_sem=drecv.at[m],
            device_id=(jnp.maximum(s - 1, 0), r), device_id_type=MESH,
        )

    def dr_relay(m):
        return pltpu.make_async_remote_copy(
            src_ref=DRN.at[m], dst_ref=RD.at[m],
            send_sem=dsend.at[m], recv_sem=erecv.at[m],
            device_id=(jnp.minimum(s + ny - 1, last), r), device_id_type=MESH,
        )

    def dr_pass(m):
        return pltpu.make_async_remote_copy(
            src_ref=RD.at[m], dst_ref=DRB.at[m],
            send_sem=esend.at[m], recv_sem=drecv.at[m],
            device_id=(jnp.maximum(s - ny, 0), r), device_id_type=MESH,
        )

    def q_copy(m, i):
        q = peer(2 * i)
        return pltpu.make_async_remote_copy(
            src_ref=DQ.at[m, mine], dst_ref=DQ.at[m, mine],
            send_sem=qsend.at[m, i], recv_sem=qrecv.at[m, i],
            device_id=(s, q), device_id_type=MESH,
        )

    def q_wait(m, i):
        q = lax.rem(r - 2 * i + ndp, ndp)
        pltpu.make_async_remote_copy(
            src_ref=DQ.at[m, rows_of(q)], dst_ref=DQ.at[m, rows_of(q)],
            send_sem=qsend.at[m, i], recv_sem=qrecv.at[m, i],
            device_id=(s, q), device_id_type=MESH,
        ).wait_recv()

    def q_swap(m, rows):
        return pltpu.make_async_remote_copy(
            src_ref=DQ.at[m, rows], dst_ref=DQ.at[m, rows],
            send_sem=qsend.at[m, 0], recv_sem=qrecv.at[m, 0],
            device_id=(s, core), device_id_type=MESH,
        )

    def both(q):
        return pl.ds(2 * (q // 2), 2)

    def y_copy(m, i):
        q = peer(2 * i)
        return pltpu.make_async_remote_copy(
            src_ref=DY.at[m, both(q)], dst_ref=DS.at[m, :, mine],
            send_sem=ysend.at[m, i], recv_sem=yrecv.at[m, i],
            device_id=(s, q), device_id_type=MESH,
        )

    def y_wait(m, i):
        q = lax.rem(r - 2 * i + ndp, ndp)
        pltpu.make_async_remote_copy(
            src_ref=DY.at[m, both(q)], dst_ref=DS.at[m, :, rows_of(q)],
            send_sem=ysend.at[m, i], recv_sem=yrecv.at[m, i],
            device_id=(s, q), device_id_type=MESH,
        ).wait_recv()

    def y_swap(m, which, rows):
        return pltpu.make_async_remote_copy(
            src_ref=DS.at[m, which, rows], dst_ref=DS.at[m, which, rows],
            send_sem=ysend.at[m, 0], recv_sem=yrecv.at[m, 0],
            device_id=(s, core), device_id_type=MESH,
        )

    @pl.when(s == last)
    def _():
        for i in range(ndp):
            pltpu.make_async_copy(
                out_grad.at[:, :, pl.ds(i * blk, blk)], DY.at[:, i], outsem.at[i]
            ).wait()

    def settle(m):
        q_swap(m, foreign).wait_recv()
        y_swap(m, c, foreign).wait_recv()
        GI[...] += dot_tn(XS[m], DQ[m])
        GO[...] += dot_tn(DS[m, c], RA[m])

    def exchange_q(m):
        for i in range(1, ndp // 2):
            q_copy(m, i).start()

    def exchange_y(m):
        for i in range(1, ndp // 2):
            y_copy(m, i).start()

    def exchange(m):
        exchange_q(m)
        exchange_y(m)

    inline = s < nsec // 4

    def step(m, carry):
        @pl.when(direct)
        def _():
            for k in range(nchunk):
                pl.when(s < last)(chunk_copy(m, k).wait_recv)
            rows = jnp.concatenate([DY[m, j] for j in range(ndp)], axis=1)
            DRB[m] = dot(rows, WS[...].reshape(width, cols)).astype(BF)

        pl.when(s < first)(dr_copy(m).wait_recv)
        d_mixed = DRB[m]
        parts = [[], [], []]
        for h in range(heads):
            q = QKV[m, :, h * hd : (h + 1) * hd]
            k = QKV[m, :, cols + h * hd : cols + (h + 1) * hd]
            v = QKV[m, :, 2 * cols + h * hd : 2 * cols + (h + 1) * hd]
            dr = d_mixed[:, h * hd : (h + 1) * hd]
            d_score = (dot_nt(dr, v) * TAB[h]).astype(BF)
            parts[0].append(dot(d_score, k).astype(BF))
            parts[1].append(dot_tn(d_score, q).astype(BF))
            parts[2].append(dot_tn(SC[m, h], dr).astype(BF))
        d_all = jnp.concatenate(parts[0] + parts[1] + parts[2], axis=1)

        DQ[m, mine] = (d_all.astype(F32) * live).astype(BF)
        pl.when(s == 0)(functools.partial(exchange_q, m))
        total = dot(d_all, MM[...])
        for k in range(nchunk):
            pl.when(s < first)(chunk_copy(m, k).wait_recv)
            if k == nchunk - 1:
                pl.when(s == 0)(functools.partial(exchange_y, m))
            span = range(k * per, (k + 1) * per)
            rows = jnp.concatenate([DY[m, j] for j in span], axis=1)
            total += dot(rows, WO[k * per : (k + 1) * per].reshape(per * blk, cols))
            if k == nchunk - 1:
                DRN[m] = total.astype(BF)
                pl.when(ahead & to_next)(dr_copy(m).start)
                pl.when(ahead & to_relay)(dr_relay(m).start)
            for j in span:
                back = dot(d_all, WT[j])
                NX[m, j] = (DY[m, j].astype(F32) + back).astype(BF)

            @pl.when(to_next)
            def _():
                chunk_copy(m, k).start()

            @pl.when(to_relay)
            def _():
                relay_copy(m, k).start()

        DS[m, :, mine] = DY[m, both(r)]

        @pl.when(inline & (s > 0))
        def _():
            exchange(m)

        return carry

    lax.fori_loop(0, micro, step, 0)
    writes = [
        pltpu.make_async_copy(
            NX.at[:, i], in_grad.at[0, :, :, pl.ds(i * blk, blk)], outsem.at[i]
        )
        for i in range(ndp)
    ]
    for copy in writes:
        copy.start()

    @pl.when(node)
    def _():
        def forward(m, carry):
            for k in range(nchunk):
                if k == nchunk - 1:
                    dr_relay(m).wait_recv()
                    dr_pass(m).start()
                relay_copy(m, k).wait_recv()
                pass_on(m, k).start()
            return carry

        lax.fori_loop(0, micro, forward, 0)

    pl.when(s >= last - lead)(exchange_early)

    @pl.when(s >= nsec // 4)
    def _():
        def send(m, carry):
            exchange(m)
            return carry

        lax.fori_loop(0, micro, send, 0)

    scale = 1.0 / (ndp - 1.0)

    def swap(m):
        for i in range(1, ndp // 2):
            q_wait(m, i)
        q_swap(m, plane).start()
        for i in range(1, ndp // 2):
            y_wait(m, i)
        y_swap(m, 1 - c, plane).start()

    swap(0)

    def finish(m, carry):
        swap(m + 1)
        settle(m)
        return carry

    lax.fori_loop(0, micro - 1, finish, 0)
    m = micro - 1
    y_swap(m, c, foreign).wait_recv()
    GO[...] = (GO[...] + dot_tn(DS[m, c], RA[m])) * scale
    out1 = pltpu.make_async_copy(GO, grad_out.at[0], loc.at[1])
    out1.start()
    q_swap(m, foreign).wait_recv()
    GI[...] = (GI[...] + dot_tn(XS[m], DQ[m])) * scale
    out2 = pltpu.make_async_copy(GI, grad_in.at[0], loc.at[2])
    out2.start()

    def drain(m, carry):
        pl.when(ahead)(dr_copy(m).wait_send)

        @pl.when(s > 0)
        def _():
            for k in range(nchunk):
                chunk_copy(m, k).wait_send()

        @pl.when(node)
        def _():
            dr_pass(m).wait_send()
            for k in range(nchunk):
                pass_on(m, k).wait_send()

        for i in range(1, ndp // 2):
            q_copy(m, i).wait_send()
        q_swap(m, plane).wait_send()
        for i in range(1, ndp // 2):
            y_copy(m, i).wait_send()
        y_swap(m, 1 - c, plane).wait_send()
        return carry

    lax.fori_loop(0, micro, drain, 0)
    for copy in writes:
        copy.wait()
    out1.wait()
    out2.wait()


def shards(acts, out_grad, w_in, w_out, decay_rate, cycle_order):
    nsec = lax.axis_size("section")
    ndp = lax.axis_size("dp")
    _, micro, tok, width = acts.shape
    cols = w_out.shape[2]
    heads = decay_rate.shape[1]
    hd = cols // heads
    blk = width // ndp
    nchunk = 2
    dims = (nsec, ndp, micro, tok, width, heads, hd, nchunk)
    dma = pltpu.SemaphoreType.DMA
    any_spec = pl.BlockSpec(memory_space=pl.ANY)
    smem = pl.BlockSpec(memory_space=pltpu.SMEM)
    return pl.pallas_call(
        functools.partial(kernel, dims),
        name="retention_stack_back",
        out_shape=(
            jax.ShapeDtypeStruct((1, micro, tok, width), BF),
            jax.ShapeDtypeStruct((1, blk, 3 * cols), F32),
            jax.ShapeDtypeStruct((1, blk, cols), F32),
        ),
        in_specs=[any_spec] * 4 + [smem] * 2,
        out_specs=[any_spec] * 3,
        scratch_shapes=[
            pltpu.VMEM((ndp, blk, 3 * cols), BF),
            pltpu.VMEM((ndp, blk, cols), BF),
            pltpu.VMEM((ndp, blk, cols), BF),
            pltpu.VMEM((ndp, 3 * cols, blk), BF),
            pltpu.VMEM((3 * cols, cols), F32),
            pltpu.VMEM((3 * cols, cols), BF),
            pltpu.VMEM((micro, tok, cols), BF),
            pltpu.VMEM((micro, tok, cols), BF),
            pltpu.VMEM((micro, tok, cols), BF),
            pltpu.VMEM((ndp, micro, tok, blk), BF),
            pltpu.VMEM((micro, ndp, tok, blk), BF),
            pltpu.VMEM((micro, ndp, tok, blk), BF),
            pltpu.VMEM((micro, ndp, tok, blk), BF),
            pltpu.VMEM((micro * tok, 3 * cols), F32),
            pltpu.VMEM((micro, tok, 3 * cols), BF),
            pltpu.VMEM((micro, heads, tok, tok), BF),
            pltpu.VMEM((heads, tok, tok), F32),
            pltpu.VMEM((micro, ndp * tok, blk), BF),
            pltpu.VMEM((micro, 2, ndp * tok, blk), BF),
            pltpu.VMEM((micro, ndp * tok, 3 * cols), BF),
            pltpu.VMEM((micro, ndp * tok, cols), BF),
            pltpu.VMEM((blk, 3 * cols), F32),
            pltpu.VMEM((blk, cols), F32),
            dma((4 + ndp,)),
            dma((96,)),
            dma((ndp, 2, 3)),
            dma((micro, nchunk)),
            dma((micro, nchunk)),
            dma((micro, nchunk)),
            dma((micro, nchunk)),
            dma((micro,)),
            dma((micro,)),
            dma((micro,)),
            dma((micro,)),
            dma((ndp,)),
            dma((ndp,)),
            dma((ndp // 2,)),
            dma((ndp // 2,)),
            dma((micro, ndp // 2)),
            dma((micro, ndp // 2)),
            dma((micro, ndp // 2)),
            dma((micro, ndp // 2)),
            dma((ndp,)),
        ],
        compiler_params=pltpu.CompilerParams(
            collective_id=0, has_side_effects=True, vmem_limit_bytes=60 * 1024 * 1024
        ),
        cost_estimate=pl.CostEstimate(
            flops=6_000_000_000, bytes_accessed=8_000_000, transcendentals=4096
        ),
    )(acts, out_grad, w_in, w_out, decay_rate, cycle_order)


def solution(mesh):
    placed = (
        P("section", None, "dp", None),
        P(None, "dp", None),
        P("section", "dp", None),
        P("section", "dp", None),
        P("section", None),
        P(),
    )
    return jax.shard_map(
        shards,
        mesh=mesh,
        in_specs=placed,
        out_specs=(
            P("section", None, "dp", None),
            P("section", "dp", None),
            P("section", "dp", None),
        ),
        check_vma=False,
    )
```

```python
import functools

import jax
import jax.numpy as jnp
from jax import lax
from jax.experimental import pallas as pl
from jax.experimental.pallas import tpu as pltpu
from jax.sharding import PartitionSpec as P

MESH = pl.DeviceIdType.MESH
BF = jnp.bfloat16
F32 = jnp.float32


def dot(a, b):
    return jnp.dot(a, b, preferred_element_type=F32)


def dot_nt(a, b):
    return lax.dot_general(a, b, (((1,), (1,)), ((), ())), preferred_element_type=F32)


def dot_tn(a, b):
    return lax.dot_general(a, b, (((0,), (0,)), ((), ())), preferred_element_type=F32)


def kernel(
    dims,
    acts, out_grad, w_in, w_out, rates, order,
    in_grad, grad_in, grad_out,
    WI, WS, WO, WT, MA, MM, DRB, DRN, RD, XB, DY, NX, RB, ACC, QKV, SC, TAB, XS, DS, DQ, RA, GI, GO,
    loc, wsend, wrecv, csend, crecv, bsend, brecv, dsend, drecv, esend, erecv, xsend, xrecv, rsend, rrecv, qsend, qrecv, ysend, yrecv, outsem,
):
    nsec, ndp, micro, tok, width, heads, hd, nchunk = dims
    cols = heads * hd
    blk = width // ndp
    half = blk // 2
    per = ndp // nchunk
    nx = ndp // 4
    s = lax.axis_index("section")
    r = lax.axis_index("dp")
    x, zl, c = r // 4, (r // 2) % 2, r % 2
    last = nsec - 1
    lead = min(4, nsec // 4)
    ny = 4 if nsec >= 16 else 2
    y = lax.rem(s, ny)
    first = last - 2
    direct = s >= first
    ahead = (s > 0) & (s <= first)
    to_relay = (s > 0) & (y == 0) & (zl == 0)
    to_next = (s > 0) & ((y != 0) | (zl != 0))
    node = (s >= ny) & (y == ny - 1) & (zl == 0)
    by_relay = (s < last) & (y == ny - 1) & (zl == 0)
    by_prev = (s < last) & ((y != ny - 1) | (zl != 0))
    slot = c * (ndp // 2) + r // 2

    def rep(xx, zz, cc):
        return lax.rem(xx + nx, nx) * 4 + zz * 2 + cc

    core, zp = rep(x, zl, 1 - c), rep(x, 1 - zl, c)
    xp, xm, xo = rep(x + 1, zl, c), rep(x - 1, zl, c), rep(x + 2, zl, c)
    xpz, xmz, xoz = rep(x + 1, 1 - zl, c), rep(x - 1, 1 - zl, c), rep(x + 2, 1 - zl, c)

    def peer(i):
        return lax.rem(r + i, ndp)

    def slot_of(q):
        return lax.rem(q, 2) * (ndp // 2) + q // 2

    local = [
        pltpu.make_async_copy(w_in.at[0], WI.at[r], loc.at[0]),
        pltpu.make_async_copy(w_out.at[0], WS.at[r], loc.at[1]),
    ]
    for i in range(ndp):
        local.append(
            pltpu.make_async_copy(
                acts.at[0, :, :, pl.ds(i * blk, blk)], XB.at[i], loc.at[2 + i]
            )
        )
    for copy in local:
        copy.start()

    barrier = pltpu.get_barrier_semaphore()
    for i in range(1, ndp):
        pl.semaphore_signal(barrier, inc=1, device_id=(s, peer(i)), device_id_type=MESH)

    def greet(cond, section):
        @pl.when(cond)
        def _():
            pl.semaphore_signal(
                barrier, inc=1, device_id=(section, r), device_id_type=MESH
            )

    greet(by_prev, jnp.minimum(s + 1, last))
    greet(by_relay, jnp.minimum(s + ny, last))
    greet(node, jnp.maximum(s - (ny - 1), 0))
    greet(ahead, jnp.maximum(s - 1, 0))
    receivers = (
        jnp.where(to_next, 1, 0)
        + jnp.where(to_relay, 1, 0)
        + jnp.where(node, 1, 0)
        + jnp.where(s < first, 1, 0)
    )
    pl.semaphore_wait(barrier, ndp - 1 + receivers)

    def piece(ref, q, h):
        return ref.at[q, pl.ds(h * half, half)]

    sent = []
    needed = (s >= 0, direct, ahead)

    def push(q, h, target, arrays=(0, 1, 2), own=False):
        for which in arrays:
            ref = (WI, WS, WO)[which]
            src = piece(ref, q, h)
            if own and which < 2:
                src = (w_in, w_out)[which].at[0, pl.ds(h * half, half)]
            copy = pltpu.make_async_remote_copy(
                src_ref=src,
                dst_ref=piece(ref, q, h),
                send_sem=wsend.at[len(sent)],
                recv_sem=wrecv.at[q, h, which],
                device_id=(s, target),
                device_id_type=MESH,
            )
            sent.append((copy, needed[which]))
            pl.when(needed[which])(copy.start)

    def arrive(q, h):
        for which, ref in enumerate((WI, WS, WO)):
            copy = pltpu.make_async_remote_copy(
                src_ref=piece(ref, q, h),
                dst_ref=piece(ref, q, h),
                send_sem=wsend.at[0],
                recv_sem=wrecv.at[q, h, which],
                device_id=(s, core),
                device_id_type=MESH,
            )
            pl.when(needed[which])(copy.wait_recv)

    def up_copy(h):
        return pltpu.make_async_remote_copy(
            src_ref=w_out.at[0, pl.ds(h * half, half)],
            dst_ref=piece(WO, r, h),
            send_sem=loc.at[2 + ndp + h],
            recv_sem=wrecv.at[r, h, 2],
            device_id=(jnp.minimum(s + 1, last), r),
            device_id_type=MESH,
        )

    for h in range(2):
        pl.when(s < first)(up_copy(h).start)
    for h in range(2):
        for target in (xp, xm, zp, core):
            push(r, h, target, arrays=(0, 1), own=True)

    MA[...] = jnp.zeros_like(MA)
    ACC[...] = jnp.zeros_like(ACC)

    def fold(q):
        MA[...] += dot(WT[q], WO[q])

    def add(q):
        ACC[...] += dot(XB[q].reshape(micro * tok, blk), WI[q])
        WT[q] = WI[q].T
        pl.when(ahead)(functools.partial(fold, q))

    for copy in local:
        copy.wait()

    @pl.when(s == last)
    def _():
        for i in range(ndp):
            pltpu.make_async_copy(
                out_grad.at[:, :, pl.ds(i * blk, blk)], DY.at[:, i], outsem.at[i]
            ).start()

    spot_t = lax.broadcasted_iota(jnp.int32, (tok, tok), 0)
    spot_j = lax.broadcasted_iota(jnp.int32, (tok, tok), 1)
    offset = (spot_t - spot_j).astype(F32)
    for h in range(heads):
        decayed = jnp.exp(-rates[0, h] * jnp.maximum(offset, 0.0))
        TAB[h] = jnp.where(offset >= 0.0, decayed, 0.0) / hd

    @pl.when(ahead)
    def _():
        for h in range(2):
            up_copy(h).wait_recv()

    for h in range(2):
        for target in (xp, xm, zp, core):
            push(r, h, target, arrays=(2,))
    add(r)
    arrive(xm, 0)
    push(xm, 0, xp)
    push(xm, 0, core)
    arrive(xp, 0)
    push(xp, 0, core)
    arrive(zp, 0)
    push(zp, 0, xp)
    push(zp, 0, xm)
    push(zp, 0, core)
    arrive(core, 0)
    arrive(core, 1)
    add(core)
    arrive(xp, 1)
    push(xp, 1, xm)
    push(xp, 1, core)
    arrive(xm, 1)
    push(xm, 1, core)
    arrive(zp, 1)
    push(zp, 1, xp)
    push(zp, 1, xm)
    push(zp, 1, core)
    add(xm)
    add(xp)
    add(zp)
    arrive(xo, 0)
    push(xo, 0, zp)
    push(xo, 0, core)
    arrive(xo, 1)
    push(xo, 1, zp)
    push(xo, 1, core)

    def other(q):
        return q + 1 - 2 * c

    for q in (xm, xp, zp):
        arrive(other(q), 0)
        arrive(other(q), 1)
        add(other(q))
    add(xo)
    for q in (xmz, xpz):
        for h in range(2):
            arrive(q, h)
            push(q, h, core)
    arrive(xoz, 0)
    push(xoz, 0, core)
    add(xmz)
    add(xpz)
    arrive(xoz, 1)
    push(xoz, 1, core)
    for q in (xo, xmz, xpz):
        arrive(other(q), 0)
        arrive(other(q), 1)
        add(other(q))
    add(xoz)
    arrive(other(xoz), 0)
    arrive(other(xoz), 1)
    add(other(xoz))

    @pl.when(ahead)
    def _():
        MM[...] = MA[...].astype(BF)

    failed = order[ndp - 1]
    live = jnp.where(r == failed, 0.0, 1.0).astype(F32)
    mine = pl.ds(pl.multiple_of(slot * tok, tok), tok)

    QKV[...] = ACC[...].astype(BF).reshape(micro, tok, 3 * cols)
    for m in range(micro):
        for h in range(heads):
            q = QKV[m, :, h * hd : (h + 1) * hd]
            k = QKV[m, :, cols + h * hd : cols + (h + 1) * hd]
            SC[m, h] = (dot_nt(q, k) * TAB[h]).astype(BF)

    plane = pl.ds(pl.multiple_of(c * (ndp // 2) * tok, tok), (ndp // 2) * tok)
    foreign = pl.ds(pl.multiple_of((1 - c) * (ndp // 2) * tok, tok), (ndp // 2) * tok)

    def rows_of(q):
        return pl.ds(pl.multiple_of(slot_of(q) * tok, tok), tok)

    def x_copy(i):
        q = peer(i)
        return pltpu.make_async_remote_copy(
            src_ref=XB.at[q], dst_ref=XS.at[:, mine],
            send_sem=xsend.at[i], recv_sem=xrecv.at[i],
            device_id=(s, q), device_id_type=MESH,
        )

    def x_wait(i):
        q = lax.rem(r - i + ndp, ndp)
        pltpu.make_async_remote_copy(
            src_ref=XB.at[q], dst_ref=XS.at[:, rows_of(q)],
            send_sem=xsend.at[i], recv_sem=xrecv.at[i],
            device_id=(s, q), device_id_type=MESH,
        ).wait_recv()

    def r_copy(i):
        q = peer(2 * i)
        return pltpu.make_async_remote_copy(
            src_ref=RA.at[:, mine], dst_ref=RA.at[:, mine],
            send_sem=rsend.at[i], recv_sem=rrecv.at[i],
            device_id=(s, q), device_id_type=MESH,
        )

    def r_wait(i):
        q = lax.rem(r - 2 * i + ndp, ndp)
        pltpu.make_async_remote_copy(
            src_ref=RA.at[:, rows_of(q)], dst_ref=RA.at[:, rows_of(q)],
            send_sem=rsend.at[i], recv_sem=rrecv.at[i],
            device_id=(s, q), device_id_type=MESH,
        ).wait_recv()

    def r_swap(rows):
        return pltpu.make_async_remote_copy(
            src_ref=RA.at[:, rows], dst_ref=RA.at[:, rows],
            send_sem=rsend.at[0], recv_sem=rrecv.at[0],
            device_id=(s, core), device_id_type=MESH,
        )

    own_x = pltpu.make_async_copy(XB.at[r], XS.at[:, mine], loc.at[0])

    def exchange_early():
        for m in range(micro):
            for h in range(heads):
                v = QKV[m, :, 2 * cols + h * hd : 2 * cols + (h + 1) * hd]
                mixed = dot(SC[m, h], v).astype(BF)
                RA[m, mine, h * hd : (h + 1) * hd] = (mixed.astype(F32) * live).astype(BF)
        for i in range(1, ndp // 2):
            r_copy(i).start()
        own_x.start()
        for i in range(1, ndp):
            x_copy(i).start()
        for i in range(1, ndp // 2):
            r_wait(i)
        r_swap(plane).start()
        own_x.wait()
        for i in range(1, ndp):
            x_wait(i)
        r_swap(foreign).wait_recv()
        for i in range(1, ndp):
            x_copy(i).wait_send()
        for i in range(1, ndp // 2):
            r_copy(i).wait_send()
        r_swap(plane).wait_send()
        for copy, cond in sent:
            pl.when(cond)(copy.wait_send)
        for h in range(2):
            pl.when(s < first)(up_copy(h).wait_send)

    GI[...] = jnp.zeros_like(GI)
    GO[...] = jnp.zeros_like(GO)
    early = s < last - lead
    pl.when(early)(exchange_early)

    def chunk_copy(m, k):
        part = pl.ds(k * per, per)
        return pltpu.make_async_remote_copy(
            src_ref=NX.at[m, part], dst_ref=DY.at[m, part],
            send_sem=csend.at[m, k], recv_sem=crecv.at[m, k],
            device_id=(jnp.maximum(s - 1, 0), r), device_id_type=MESH,
        )

    def relay_copy(m, k):
        part = pl.ds(k * per, per)
        return pltpu.make_async_remote_copy(
            src_ref=NX.at[m, part], dst_ref=RB.at[m, part],
            send_sem=csend.at[m, k], recv_sem=brecv.at[m, k],
            device_id=(jnp.minimum(s + ny - 1, last), r), device_id_type=MESH,
        )

    def pass_on(m, k):
        part = pl.ds(k * per, per)
        return pltpu.make_async_remote_copy(
            src_ref=RB.at[m, part], dst_ref=DY.at[m, part],
            send_sem=bsend.at[m, k], recv_sem=crecv.at[m, k],
            device_id=(jnp.maximum(s - ny, 0), r), device_id_type=MESH,
        )

    def dr_copy(m):
        return pltpu.make_async_remote_copy(
            src_ref=DRN.at[m], dst_ref=DRB.at[m],
            send_sem=dsend.at[m], recv_sem=drecv.at[m],
            device_id=(jnp.maximum(s - 1, 0), r), device_id_type=MESH,
        )

    def dr_relay(m):
        return pltpu.make_async_remote_copy(
            src_ref=DRN.at[m], dst_ref=RD.at[m],
            send_sem=dsend.at[m], recv_sem=erecv.at[m],
            device_id=(jnp.minimum(s + ny - 1, last), r), device_id_type=MESH,
        )

    def dr_pass(m):
        return pltpu.make_async_remote_copy(
            src_ref=RD.at[m], dst_ref=DRB.at[m],
            send_sem=esend.at[m], recv_sem=drecv.at[m],
            device_id=(jnp.maximum(s - ny, 0), r), device_id_type=MESH,
        )

    def q_copy(m, i):
        q = peer(2 * i)
        return pltpu.make_async_remote_copy(
            src_ref=DQ.at[m, mine], dst_ref=DQ.at[m, mine],
            send_sem=qsend.at[m, i], recv_sem=qrecv.at[m, i],
            device_id=(s, q), device_id_type=MESH,
        )

    def q_wait(m, i):
        q = lax.rem(r - 2 * i + ndp, ndp)
        pltpu.make_async_remote_copy(
            src_ref=DQ.at[m, rows_of(q)], dst_ref=DQ.at[m, rows_of(q)],
            send_sem=qsend.at[m, i], recv_sem=qrecv.at[m, i],
            device_id=(s, q), device_id_type=MESH,
        ).wait_recv()

    def q_swap(m, rows):
        return pltpu.make_async_remote_copy(
            src_ref=DQ.at[m, rows], dst_ref=DQ.at[m, rows],
            send_sem=qsend.at[m, 0], recv_sem=qrecv.at[m, 0],
            device_id=(s, core), device_id_type=MESH,
        )

    def both(q):
        return pl.ds(2 * (q // 2), 2)

    def y_copy(m, i):
        q = peer(2 * i)
        return pltpu.make_async_remote_copy(
            src_ref=DY.at[m, both(q)], dst_ref=DS.at[m, :, mine],
            send_sem=ysend.at[m, i], recv_sem=yrecv.at[m, i],
            device_id=(s, q), device_id_type=MESH,
        )

    def y_wait(m, i):
        q = lax.rem(r - 2 * i + ndp, ndp)
        pltpu.make_async_remote_copy(
            src_ref=DY.at[m, both(q)], dst_ref=DS.at[m, :, rows_of(q)],
            send_sem=ysend.at[m, i], recv_sem=yrecv.at[m, i],
            device_id=(s, q), device_id_type=MESH,
        ).wait_recv()

    def y_swap(m, which, rows):
        return pltpu.make_async_remote_copy(
            src_ref=DS.at[m, which, rows], dst_ref=DS.at[m, which, rows],
            send_sem=ysend.at[m, 0], recv_sem=yrecv.at[m, 0],
            device_id=(s, core), device_id_type=MESH,
        )

    @pl.when(s == last)
    def _():
        for i in range(ndp):
            pltpu.make_async_copy(
                out_grad.at[:, :, pl.ds(i * blk, blk)], DY.at[:, i], outsem.at[i]
            ).wait()

    def settle(m):
        q_swap(m, foreign).wait_recv()
        y_swap(m, c, foreign).wait_recv()
        GI[...] += dot_tn(XS[m], DQ[m])
        GO[...] += dot_tn(DS[m, c], RA[m])

    def exchange_q(m):
        for i in range(1, ndp // 2):
            q_copy(m, i).start()

    def exchange_y(m):
        for i in range(1, ndp // 2):
            y_copy(m, i).start()

    def exchange(m):
        exchange_q(m)
        exchange_y(m)

    inline = s < max(1, nsec // 5)

    def step(m, carry):
        @pl.when(direct)
        def _():
            for k in range(nchunk):
                pl.when(s < last)(chunk_copy(m, k).wait_recv)
            rows = jnp.concatenate([DY[m, j] for j in range(ndp)], axis=1)
            DRB[m] = dot(rows, WS[...].reshape(width, cols)).astype(BF)

        pl.when(s < first)(dr_copy(m).wait_recv)
        d_mixed = DRB[m]
        parts = [[], [], []]
        for h in range(heads):
            q = QKV[m, :, h * hd : (h + 1) * hd]
            k = QKV[m, :, cols + h * hd : cols + (h + 1) * hd]
            v = QKV[m, :, 2 * cols + h * hd : 2 * cols + (h + 1) * hd]
            dr = d_mixed[:, h * hd : (h + 1) * hd]
            d_score = (dot_nt(dr, v) * TAB[h]).astype(BF)
            parts[0].append(dot(d_score, k).astype(BF))
            parts[1].append(dot_tn(d_score, q).astype(BF))
            parts[2].append(dot_tn(SC[m, h], dr).astype(BF))
        d_all = jnp.concatenate(parts[0] + parts[1] + parts[2], axis=1)

        DQ[m, mine] = (d_all.astype(F32) * live).astype(BF)
        pl.when(s == 0)(functools.partial(exchange_q, m))
        total = dot(d_all, MM[...])
        for k in range(nchunk):
            pl.when(s < first)(chunk_copy(m, k).wait_recv)
            if k == nchunk - 1:
                pl.when(s == 0)(functools.partial(exchange_y, m))
            span = range(k * per, (k + 1) * per)
            rows = jnp.concatenate([DY[m, j] for j in span], axis=1)
            total += dot(rows, WO[k * per : (k + 1) * per].reshape(per * blk, cols))
            if k == nchunk - 1:
                DRN[m] = total.astype(BF)
                pl.when(ahead & to_next)(dr_copy(m).start)
                pl.when(ahead & to_relay)(dr_relay(m).start)
            for j in span:
                back = dot(d_all, WT[j])
                NX[m, j] = (DY[m, j].astype(F32) + back).astype(BF)

            @pl.when(to_next)
            def _():
                chunk_copy(m, k).start()

            @pl.when(to_relay)
            def _():
                relay_copy(m, k).start()

        DS[m, :, mine] = DY[m, both(r)]

        @pl.when(inline & (s > 0))
        def _():
            exchange(m)

        return carry

    lax.fori_loop(0, micro, step, 0)
    writes = [
        pltpu.make_async_copy(
            NX.at[:, i], in_grad.at[0, :, :, pl.ds(i * blk, blk)], outsem.at[i]
        )
        for i in range(ndp)
    ]
    for copy in writes:
        copy.start()

    @pl.when(node)
    def _():
        def forward(m, carry):
            for k in range(nchunk):
                if k == nchunk - 1:
                    dr_relay(m).wait_recv()
                    dr_pass(m).start()
                relay_copy(m, k).wait_recv()
                pass_on(m, k).start()
            return carry

        lax.fori_loop(0, micro, forward, 0)

    pl.when(s >= last - lead)(exchange_early)

    @pl.when(s >= max(1, nsec // 5))
    def _():
        def send(m, carry):
            exchange(m)
            return carry

        lax.fori_loop(0, micro, send, 0)

    scale = 1.0 / (ndp - 1.0)

    def swap(m):
        for i in range(1, ndp // 2):
            q_wait(m, i)
        q_swap(m, plane).start()
        for i in range(1, ndp // 2):
            y_wait(m, i)
        y_swap(m, 1 - c, plane).start()

    def drain(m):
        pl.when(ahead)(dr_copy(m).wait_send)

        @pl.when(s > 0)
        def _():
            for k in range(nchunk):
                chunk_copy(m, k).wait_send()

        @pl.when(node)
        def _():
            dr_pass(m).wait_send()
            for k in range(nchunk):
                pass_on(m, k).wait_send()

        for i in range(1, ndp // 2):
            q_copy(m, i).wait_send()
        q_swap(m, plane).wait_send()
        for i in range(1, ndp // 2):
            y_copy(m, i).wait_send()
        y_swap(m, 1 - c, plane).wait_send()

    swap(0)

    def finish(m, carry):
        swap(m + 1)
        settle(m)
        drain(m)
        return carry

    lax.fori_loop(0, micro - 1, finish, 0)
    m = micro - 1
    y_swap(m, c, foreign).wait_recv()
    GO[...] = (GO[...] + dot_tn(DS[m, c], RA[m])) * scale
    out1 = pltpu.make_async_copy(GO, grad_out.at[0], loc.at[1])
    out1.start()
    q_swap(m, foreign).wait_recv()
    GI[...] = (GI[...] + dot_tn(XS[m], DQ[m])) * scale
    out2 = pltpu.make_async_copy(GI, grad_in.at[0], loc.at[2])
    out2.start()

    drain(micro - 1)
    for copy in writes:
        copy.wait()
    out1.wait()
    out2.wait()


def shards(acts, out_grad, w_in, w_out, decay_rate, cycle_order):
    nsec = lax.axis_size("section")
    ndp = lax.axis_size("dp")
    _, micro, tok, width = acts.shape
    cols = w_out.shape[2]
    heads = decay_rate.shape[1]
    hd = cols // heads
    blk = width // ndp
    nchunk = 2
    dims = (nsec, ndp, micro, tok, width, heads, hd, nchunk)
    dma = pltpu.SemaphoreType.DMA
    any_spec = pl.BlockSpec(memory_space=pl.ANY)
    smem = pl.BlockSpec(memory_space=pltpu.SMEM)
    return pl.pallas_call(
        functools.partial(kernel, dims),
        name="retention_stack_back",
        out_shape=(
            jax.ShapeDtypeStruct((1, micro, tok, width), BF),
            jax.ShapeDtypeStruct((1, blk, 3 * cols), F32),
            jax.ShapeDtypeStruct((1, blk, cols), F32),
        ),
        in_specs=[any_spec] * 4 + [smem] * 2,
        out_specs=[any_spec] * 3,
        scratch_shapes=[
            pltpu.VMEM((ndp, blk, 3 * cols), BF),
            pltpu.VMEM((ndp, blk, cols), BF),
            pltpu.VMEM((ndp, blk, cols), BF),
            pltpu.VMEM((ndp, 3 * cols, blk), BF),
            pltpu.VMEM((3 * cols, cols), F32),
            pltpu.VMEM((3 * cols, cols), BF),
            pltpu.VMEM((micro, tok, cols), BF),
            pltpu.VMEM((micro, tok, cols), BF),
            pltpu.VMEM((micro, tok, cols), BF),
            pltpu.VMEM((ndp, micro, tok, blk), BF),
            pltpu.VMEM((micro, ndp, tok, blk), BF),
            pltpu.VMEM((micro, ndp, tok, blk), BF),
            pltpu.VMEM((micro, ndp, tok, blk), BF),
            pltpu.VMEM((micro * tok, 3 * cols), F32),
            pltpu.VMEM((micro, tok, 3 * cols), BF),
            pltpu.VMEM((micro, heads, tok, tok), BF),
            pltpu.VMEM((heads, tok, tok), F32),
            pltpu.VMEM((micro, ndp * tok, blk), BF),
            pltpu.VMEM((micro, 2, ndp * tok, blk), BF),
            pltpu.VMEM((micro, ndp * tok, 3 * cols), BF),
            pltpu.VMEM((micro, ndp * tok, cols), BF),
            pltpu.VMEM((blk, 3 * cols), F32),
            pltpu.VMEM((blk, cols), F32),
            dma((4 + ndp,)),
            dma((96,)),
            dma((ndp, 2, 3)),
            dma((micro, nchunk)),
            dma((micro, nchunk)),
            dma((micro, nchunk)),
            dma((micro, nchunk)),
            dma((micro,)),
            dma((micro,)),
            dma((micro,)),
            dma((micro,)),
            dma((ndp,)),
            dma((ndp,)),
            dma((ndp // 2,)),
            dma((ndp // 2,)),
            dma((micro, ndp // 2)),
            dma((micro, ndp // 2)),
            dma((micro, ndp // 2)),
            dma((micro, ndp // 2)),
            dma((ndp,)),
        ],
        compiler_params=pltpu.CompilerParams(
            collective_id=0, has_side_effects=True, vmem_limit_bytes=60 * 1024 * 1024
        ),
        cost_estimate=pl.CostEstimate(
            flops=6_000_000_000, bytes_accessed=8_000_000, transcendentals=4096
        ),
    )(acts, out_grad, w_in, w_out, decay_rate, cycle_order)


def solution(mesh):
    placed = (
        P("section", None, "dp", None),
        P(None, "dp", None),
        P("section", "dp", None),
        P("section", "dp", None),
        P("section", None),
        P(),
    )
    return jax.shard_map(
        shards,
        mesh=mesh,
        in_specs=placed,
        out_specs=(
            P("section", None, "dp", None),
            P("section", "dp", None),
            P("section", "dp", None),
        ),
        check_vma=False,
    )
```
